128 devices in a mesh: queue: 32 (over z, y, core), tp: 4 (over x).
Axes of the slice: x: 4, y: 4, z: 4, core: 2. Of those that a mesh axis runs over, the one named last changes fastest.
Arguments:
- latents: bfloat16 [16384, 5120], P('queue'), may hold values from -6 to 6
- noise_level: int32 [64], P('queue'), may hold values from 0 to 31
- lookback: int32 [64], P('queue'), may hold values from 0 to 3, as said below
- level_table: bfloat16 [32, 10240], replicated, may hold values from -3 to 3
- w_query: bfloat16 [5120, 2560], P(None, 'tp'), may hold values from -0.078125 to 0.078125
- w_key: bfloat16 [5120, 2560], P(None, 'tp'), may hold values from -0.078125 to 0.078125
- w_value: bfloat16 [5120, 2560], P(None, 'tp'), may hold values from -0.3125 to 0.3125
- gain_query: float32 [2560], P('tp'), may hold values from 0.5 to 10
- gain_key: float32 [2560], P('tp'), may hold values from 0.5 to 10
Outputs:
- mixed: bfloat16 [16384, 2560], P('queue', 'tp')
The draws below stay inside these ranges and needn't reach their ends.
Inputs may be any that keep to these rules, and one draw needn't show every extreme that they name: lookback[f] is at most f and at most 3; some frame has exactly 3.
All inputs are finite; a program needn't handle non-finite values.
Results may differ from the reference program's by a relative error of at most 0.015.
The reference program's roundings to bfloat16 on the way count: a program that leaves them out, or rounds other values in their place, can miss the bound.
Values may be sent and summed in bfloat16 or wider, within the bound.
No kernel may reach another device: no remote copies, remote signals or barrier semaphores. Data moves between devices by JAX's collectives and lax.ppermute only.
A program may use at most 128 MiB of HBM per device.

```python
import jax
import jax.numpy as jnp
from jax import lax

D = 5120
HEADS = 20
HD = 128
WIN = 4
TPF = 256
LEVELS = 32
FRAMES = 64
TOKENS = 16384


def log_spread(key, lowest, highest):
    fraction = jax.random.uniform(key, (HEADS * HD,), jnp.float32)
    return jnp.exp(jnp.log(lowest) + fraction * (jnp.log(highest) - jnp.log(lowest)))


def draw_gain_query(key, part):
    key = jax.random.fold_in(key, 21)
    return log_spread(key, 0.5, 2.0)


def draw_gain_key(key, part):
    key = jax.random.fold_in(key, 37)
    return log_spread(key, 0.5, 2.0)


def draw_lookback(key, part):
    key = jax.random.fold_in(key, 11)
    first_key, second_key = jax.random.split(key)
    reaches = jax.random.randint(first_key, (FRAMES,), 0, WIN, dtype=jnp.int32)
    forced = jax.random.randint(second_key, (), WIN - 1, FRAMES, dtype=jnp.int32)
    positions = jnp.arange(FRAMES, dtype=jnp.int32)
    reaches = jnp.where(positions == forced, WIN - 1, reaches)
    return jnp.minimum(reaches, positions).astype(jnp.int32)


def plant(values, key, least, high):
    shape = values.shape
    spot = [jax.random.randint(jax.random.fold_in(key, axis), (), 0, shape[axis]) for axis in range(len(shape))]
    values = values.at[tuple(spot)].set(least)
    longest = shape.index(max(shape))
    spot[longest] = (spot[longest] + 1) % shape[longest]
    return values.at[tuple(spot)].set(high)


def shard_levels(stream_key, dims, cuts, low, top_value):
    loudness, own = 1.0, jax.random.fold_in(stream_key, 6)
    for position, parts in cuts:
        heights = jnp.exp(jax.random.uniform(jax.random.fold_in(own, position), (parts,), jnp.float32, low / len(cuts), top_value / len(cuts)))
        loudness = loudness * jnp.repeat(heights, dims[position] // parts).reshape([-1 if axis == position else 1 for axis in range(len(dims))])
    return loudness


def noise(key, shape, scale, limit, cuts=(), kind=jnp.bfloat16):
    array = jax.random.normal(key, shape, jnp.float32) * scale
    if len(cuts) > 0:
        array = shard_levels(key, shape, cuts, -0.22, 0.18) * array
    return jnp.clip(array, min=-limit, max=limit).astype(kind)


def setup_inputs(seed: int = 0) -> dict:
    arg_keys = jax.random.split(jax.random.key(seed), 10)
    return {
        "latents": noise(arg_keys[0], (TOKENS, D), 1.0, 6.0, ((0, 32),)),
        "noise_level": plant(jax.random.randint(arg_keys[1], (FRAMES,), 0, LEVELS), jax.random.fold_in(arg_keys[1], 1), 0, LEVELS - 1).astype(jnp.int32),
        "lookback": draw_lookback(jax.random.fold_in(arg_keys[9], 71), 0),
        "level_table": noise(arg_keys[3], (LEVELS, 2 * D), 0.5, 3.0),
        "w_query": noise(arg_keys[4], (D, HEADS * HD), D ** -0.5, 0.078125, ((1, 4),)),
        "w_key": noise(arg_keys[5], (D, HEADS * HD), D ** -0.5, 0.078125, ((1, 4),)),
        "w_value": noise(arg_keys[6], (D, HEADS * HD), (D // 16) ** -0.5, 0.3125, ((1, 4),)),
        "gain_query": draw_gain_query(jax.random.fold_in(arg_keys[9], 71), 0),
        "gain_key": draw_gain_key(jax.random.fold_in(arg_keys[9], 71), 0),
    }


EPSILON = 1e-06

def level_rows(noise_level, level_table):
    choose = (noise_level[:, None] == lax.broadcasted_iota(jnp.int32, (noise_level.shape[0], level_table.shape[0]), 1)).astype(jnp.bfloat16)
    return jnp.dot(choose, level_table, preferred_element_type=jnp.float32)

def modulate(latents, modulation, frame_count, frame_rows, model_width):
    shaped = latents.astype(jnp.float32).reshape(frame_count, frame_rows, model_width)
    center = lax.optimization_barrier(jnp.mean(shaped, axis=2, keepdims=True))
    spread = lax.optimization_barrier(jnp.mean(jnp.square(shaped - center), axis=2, keepdims=True))
    normed = (shaped - center) * lax.rsqrt(spread + EPSILON)
    shifts = modulation[:, None, :model_width]
    scales = modulation[:, None, model_width:]
    result = normed * (1.0 + scales) + shifts
    return result.reshape(frame_count * frame_rows, model_width).astype(jnp.bfloat16)

def window_attend(queries, keys_win, values_win, reach):
    frame_rows = queries.shape[0]
    head_count = queries.shape[1] // HD
    queries_h = queries.astype(jnp.float32).reshape(frame_rows, head_count, HD)
    keys_h = keys_win.astype(jnp.float32).reshape(keys_win.shape[0], head_count, HD)
    values_h = values_win.astype(jnp.float32).reshape(values_win.shape[0], head_count, HD)
    scores = jnp.einsum('qhd,khd->hqk', queries_h, keys_h) * HD ** (-0.5)
    offsets = WIN - 1 - lax.broadcasted_iota(jnp.int32, (1, 1, keys_win.shape[0]), 2) // frame_rows
    scores = jnp.where(offsets <= reach, scores, -1e+30)
    highest = lax.optimization_barrier(jnp.max(scores, axis=2, keepdims=True))
    expo = jnp.exp(scores - highest)
    chance = (expo / lax.optimization_barrier(jnp.sum(expo, axis=2, keepdims=True))).astype(jnp.bfloat16)
    result = jnp.einsum('hqk,khd->qhd', chance.astype(jnp.float32), values_h)
    return result.reshape(frame_rows, head_count * HD).astype(jnp.bfloat16)

def reference(latents, noise_level, lookback, level_table, w_query, w_key, w_value, gain_query, gain_key):
    total_cols = HEADS * HD
    modulation = level_rows(noise_level, level_table)
    shaped = modulate(latents, modulation, FRAMES, TPF, D)
    queries = jnp.dot(shaped, w_query, preferred_element_type=jnp.float32)
    keys_all = jnp.dot(shaped, w_key, preferred_element_type=jnp.float32)
    values_all = jnp.dot(shaped, w_value, preferred_element_type=jnp.float32)
    query_normed = (queries * lax.rsqrt(lax.optimization_barrier(jnp.sum(queries * queries, axis=1, keepdims=True)) / total_cols + EPSILON) * gain_query).astype(jnp.bfloat16)
    key_normed = (keys_all * lax.rsqrt(lax.optimization_barrier(jnp.sum(keys_all * keys_all, axis=1, keepdims=True)) / total_cols + EPSILON) * gain_key).astype(jnp.bfloat16)
    value_held = values_all.astype(jnp.bfloat16)
    padding = jnp.zeros(((WIN - 1) * TPF, total_cols), jnp.bfloat16)
    keys_padded = jnp.concatenate([padding, key_normed], 0)
    values_padded = jnp.concatenate([padding, value_held], 0)

    def one_frame(frame_index):
        start = frame_index * TPF
        query_rows = lax.dynamic_slice_in_dim(query_normed, start, TPF, 0)
        key_win = lax.dynamic_slice_in_dim(keys_padded, start, WIN * TPF, 0)
        value_win = lax.dynamic_slice_in_dim(values_padded, start, WIN * TPF, 0)
        reach = lax.dynamic_index_in_dim(lookback, frame_index, 0, keepdims=False)
        return window_attend(query_rows, key_win, value_win, reach)
    mixed = lax.map(one_frame, jnp.arange(FRAMES, dtype=jnp.int32))
    return mixed.reshape(TOKENS, total_cols)
```

```python
import functools

import jax
import jax.numpy as jnp
from jax import lax
from jax.experimental import pallas as pl
from jax.experimental.pallas import tpu as pltpu
from jax.sharding import PartitionSpec as P

HD = 128
WIN = 4
EPSILON = 1e-06
MIB = 2**20

ANY = pl.BlockSpec(memory_space=pl.ANY)
VMEM = pl.BlockSpec(memory_space=pltpu.VMEM)
SMEM = pl.BlockSpec(memory_space=pltpu.SMEM)


def as_rows(column):
    wide = jnp.broadcast_to(column, (column.shape[0], 128))
    parts = [
        jnp.transpose(wide[i : i + 128])[0:1] for i in range(0, column.shape[0], 128)
    ]
    return jnp.concatenate(parts, 0)


def as_columns(rows):
    parts = [
        jnp.transpose(jnp.broadcast_to(rows[i : i + 1], (128, 128)))
        for i in range(rows.shape[0])
    ]
    return jnp.concatenate(parts, 0)


def project_kernel(
    noise_level, latents, level_table, w_query, w_key, w_value,
    query_out, key_out, value_out, value_early, value_late, sums_out,
    lat, shaped_early, shaped_late, w_qk, w_v, shift, scale, query, key, value, lat_sem, w_sem, out_sem,
):
    width = latents.shape[1]
    frame = latents.shape[0] // 2
    cols = w_query.shape[1]
    lat_copies = []
    for c in range(4):
        rows = ((c // 2 + 1) % 2) * frame + (c % 2) * (frame // 2)
        copy = pltpu.make_async_copy(
            latents.at[pl.ds(rows, frame // 2)], lat.at[pl.ds(rows, frame // 2)], lat_sem.at[c]
        )
        copy.start()
        lat_copies.append(copy)
    pieces = [
        (w_key, 0, 256, w_qk, 0), (w_key, 256, 256, w_qk, 256), (w_key, 512, 128, w_qk, 512),
        (w_query, 0, 128, w_qk, 640), (w_query, 128, 256, w_qk, 768), (w_query, 384, 256, w_qk, 1024),
        (w_value, 0, 256, w_v, 0), (w_value, 256, 256, w_v, 256), (w_value, 512, 128, w_v, 512),
    ]
    w_copies = []
    for i, (src, at, size, dst, to) in enumerate(pieces):
        copy = pltpu.make_async_copy(
            src.at[:, pl.ds(at, size)], dst.at[:, pl.ds(to, size)], w_sem.at[i]
        )
        copy.start()
        w_copies.append(copy)

    for f in range(2):
        chosen = lax.broadcasted_iota(jnp.int32, (level_table.shape[0], 1), 0) == noise_level[f]
        row = jnp.sum(
            jnp.where(chosen, level_table[...].astype(jnp.float32), 0.0), axis=0, keepdims=True
        )
        shift[f : f + 1, :] = row[:, :width]
        scale[f : f + 1, :] = 1.0 + row[:, width:]

    def shape_rows(f, dst, start, count):
        x = lat[pl.ds(f * frame + start, count), :].astype(jnp.float32)
        center = jnp.mean(x, axis=1, keepdims=True)
        x = x - center
        spread = jnp.mean(x * x, axis=1, keepdims=True)
        x = x * lax.rsqrt(spread + EPSILON)
        dst[pl.ds(start, count), :] = (x * scale[f : f + 1, :] + shift[f : f + 1, :]).astype(jnp.bfloat16)

    group = 64
    for c in range(4):
        if c % 2 == 0:
            lat_copies[c // 2].wait()
        shape_rows(1, shaped_early, c * group, group)

    tiles = [
        (w_qk, 0, 256, key, 0, (0,)), (w_qk, 256, 256, key, 256, (1,)), (w_qk, 512, 256, None, 0, (2, 3)),
        (w_qk, 768, 256, query, 128, (4,)), (w_qk, 1024, 256, query, 384, (5,)),
        (w_v, 0, 256, value, 0, (6,)), (w_v, 256, 256, value, 256, (7,)), (w_v, 512, 128, value, 512, (8,)),
    ]
    waited = set()

    def tile(t, f):
        weights, at, size, dst, to, needs = tiles[t]
        for n in needs:
            if n not in waited:
                w_copies[n].wait()
                waited.add(n)
        source = shaped_early if f == 1 else shaped_late
        result = jnp.dot(
            source[...], weights[:, at : at + size], preferred_element_type=jnp.float32
        )
        rows = slice(f * frame, (f + 1) * frame)
        if dst is None:
            key[rows, 512:640] = result[:, :128]
            query[rows, 0:128] = result[:, 128:]
        else:
            dst[rows, to : to + size] = result.astype(dst.dtype)

    out_copies = []

    def send(src, dst):
        copy = pltpu.make_async_copy(src, dst, out_sem.at[len(out_copies)])
        copy.start()
        out_copies.append(copy)

    def finish(t, f):
        rows = slice(f * frame, (f + 1) * frame)
        ds = pl.ds(f * frame, frame)
        if t == 2:
            k = key[rows, :]
            sums_out[2 * f : 2 * f + 2, :] = as_rows(jnp.sum(k * k, axis=1, keepdims=True))
            send(key.at[ds], key_out.at[ds])
        if t == 4:
            q = query[rows, :]
            sums_out[4 + 2 * f : 6 + 2 * f, :] = as_rows(jnp.sum(q * q, axis=1, keepdims=True))
            send(query.at[ds], query_out.at[ds])
        if t == 7:
            send(value.at[ds], value_out.at[ds])
            send(value.at[ds], value_early if f == 1 else value_late)

    for t in range(4):
        if t % 2 == 0:
            lat_copies[2 + t // 2].wait()
        shape_rows(0, shaped_late, t * group, group)
        tile(t, 1)
        finish(t, 1)
    for t in range(4, 8):
        tile(t, 1)
        finish(t, 1)
    for t in range(8):
        tile(t, 0)
        finish(t, 0)
    for copy in out_copies:
        copy.wait()


def project(noise_level, latents, level_table, w_query, w_key, w_value):
    rows, width = latents.shape
    cols = w_query.shape[1]
    half = rows // 2
    f32, bf16 = jnp.float32, jnp.bfloat16
    return pl.pallas_call(
        project_kernel,
        out_shape=(
            jax.ShapeDtypeStruct((rows, cols), f32),
            jax.ShapeDtypeStruct((rows, cols), f32),
            jax.ShapeDtypeStruct((rows, cols), bf16),
            jax.ShapeDtypeStruct((half, cols), bf16),
            jax.ShapeDtypeStruct((half, cols), bf16),
            jax.ShapeDtypeStruct((8, 128), f32),
        ),
        in_specs=[SMEM, ANY, VMEM, ANY, ANY, ANY],
        out_specs=(ANY, ANY, ANY, ANY, ANY, VMEM),
        scratch_shapes=[
            pltpu.VMEM((rows, width), bf16),
            pltpu.VMEM((half, width), bf16),
            pltpu.VMEM((half, width), bf16),
            pltpu.VMEM((width, 2 * cols), bf16),
            pltpu.VMEM((width, cols), bf16),
            pltpu.VMEM((2, width), f32),
            pltpu.VMEM((2, width), f32),
            pltpu.VMEM((rows, cols), f32),
            pltpu.VMEM((rows, cols), f32),
            pltpu.VMEM((rows, cols), bf16),
            pltpu.SemaphoreType.DMA((4,)),
            pltpu.SemaphoreType.DMA((9,)),
            pltpu.SemaphoreType.DMA((8,)),
        ],
        compiler_params=pltpu.CompilerParams(vmem_limit_bytes=56 * MIB),
        cost_estimate=pl.CostEstimate(
            flops=2 * rows * width * 3 * cols, bytes_accessed=30_000_000, transcendentals=0
        ),
        name="project",
    )(noise_level, latents, level_table, w_query, w_key, w_value)


def norm_factor(sums, at, total_cols):
    total = sums[0][at : at + 4, :] + sums[1][at : at + 4, :] + sums[2][at : at + 4, :] + sums[3][at : at + 4, :]
    return as_columns(lax.rsqrt(total / total_cols + EPSILON))


def key_kernel(total_cols, key, gain, s0, s1, s2, s3, all_out, early, late):
    factor = norm_factor((s0, s1, s2, s3), 0, total_cols)
    half = late.shape[0]
    for c in range(0, key.shape[1], 128):
        normed = (key[:, c : c + 128] * factor * gain[0:1, c : c + 128]).astype(jnp.bfloat16)
        all_out[:, c : c + 128] = normed
        late[:, c : c + 128] = normed[:half]
        early[:, c : c + 128] = normed[half:]


def normalise_key(key, gain, sums, total_cols):
    rows, cols = key.shape
    bf16 = jnp.bfloat16
    return pl.pallas_call(
        functools.partial(key_kernel, total_cols),
        out_shape=(
            jax.ShapeDtypeStruct((rows, cols), bf16),
            jax.ShapeDtypeStruct((rows // 2, cols), bf16),
            jax.ShapeDtypeStruct((rows // 2, cols), bf16),
        ),
        in_specs=[VMEM] * 6,
        out_specs=(VMEM,) * 3,
        compiler_params=pltpu.CompilerParams(vmem_limit_bytes=24 * MIB),
        cost_estimate=pl.CostEstimate(flops=2 * rows * cols, bytes_accessed=3_000_000, transcendentals=0),
        name="normalise_key",
    )(key, gain, *sums)


def attend_block(heads, first, q, k, v, acc, peak, mass):
    for h in range(heads):
        cols = slice(h * HD, (h + 1) * HD)
        scores = lax.dot_general(
            q[:, cols], k[:, cols], (((1,), (1,)), ((), ())), preferred_element_type=jnp.float32
        ) * HD ** (-0.5)
        highest = jnp.max(scores, axis=1, keepdims=True)
        if first:
            expo = jnp.exp(scores - highest)
            mass[h] = jnp.sum(expo, axis=1, keepdims=True)
            peak[h] = highest
            acc[:, cols] = jnp.dot(
                expo.astype(jnp.bfloat16), v[:, cols], preferred_element_type=jnp.float32
            )
        else:
            before = peak[h]
            highest = jnp.maximum(highest, before)
            fade = jnp.exp(before - highest)
            expo = jnp.exp(scores - highest)
            mass[h] = mass[h] * fade + jnp.sum(expo, axis=1, keepdims=True)
            peak[h] = highest
            acc[:, cols] = acc[:, cols] * fade + jnp.dot(
                expo.astype(jnp.bfloat16), v[:, cols], preferred_element_type=jnp.float32
            )


def local_kernel(
    total_cols, info, query, gain, s0, s1, s2, s3, key, value, pair_key, pair_value,
    query_out, acc, peak, mass,
):
    factor = norm_factor((s0, s1, s2, s3), 4, total_cols)
    cols = query.shape[1]
    heads = cols // HD
    for c in range(0, cols, 128):
        query_out[:, c : c + 128] = (
            query[:, c : c + 128] * factor * gain[0:1, c : c + 128]
        ).astype(jnp.bfloat16)
    frame = query.shape[0] // 2
    at = [pl.ds(0, frame), pl.ds(frame, frame)]
    for f in range(2):
        parts = (acc.at[at[f]], peak.at[f], mass.at[f])
        q = query_out.at[at[f]]
        attend_block(heads, True, q, key.at[at[f]], value.at[at[f]], *parts)
        if f == 1:

            @pl.when(info[f] >= 1)
            def _():
                attend_block(heads, False, q, key.at[at[0]], value.at[at[0]], *parts)

        for g in range(2):

            @pl.when(jnp.logical_and(info[2] == 1, info[f] >= f + 2 - g))
            def _():
                attend_block(heads, False, q, pair_key.at[at[g]], pair_value.at[at[g]], *parts)


def local_attention(info, query, gain, sums, key, value, pair_key, pair_value, total_cols):
    rows, cols = query.shape
    heads = cols // HD
    f32 = jnp.float32
    stats = jax.ShapeDtypeStruct((2, heads, rows // 2, 1), f32)
    return pl.pallas_call(
        functools.partial(local_kernel, total_cols),
        out_shape=(
            jax.ShapeDtypeStruct((rows, cols), jnp.bfloat16),
            jax.ShapeDtypeStruct((rows, cols), f32),
            stats,
            stats,
        ),
        in_specs=[SMEM] + [VMEM] * 10,
        out_specs=(VMEM,) * 4,
        compiler_params=pltpu.CompilerParams(vmem_limit_bytes=32 * MIB),
        cost_estimate=pl.CostEstimate(flops=3_000_000_000, bytes_accessed=8_000_000, transcendentals=0),
        name="local_attention",
    )(info, query, gain, *sums, key, value, pair_key, pair_value)


def halo_kernel(
    info, query, acc_in, peak_in, mass_in, far_key, far_value, mid_key, mid_value, near_key, near_value,
    out, acc, peak, mass,
):
    heads = query.shape[1] // HD
    frame = query.shape[0] // 2
    at = [pl.ds(0, frame), pl.ds(frame, frame)]
    acc[...] = acc_in[...]
    peak[...] = peak_in[...]
    mass[...] = mass_in[...]
    for f, reach, only_first, k, v in (
        (0, 3, False, far_key, far_value),
        (0, 1, True, near_key, near_value),
        (1, 2, True, near_key, near_value),
        (0, 2, True, mid_key, mid_value),
        (1, 3, True, mid_key, mid_value),
    ):
        needed = info[f] >= reach
        if only_first:
            needed = jnp.logical_and(needed, info[2] == 0)

        @pl.when(needed)
        def _():
            attend_block(heads, False, query.at[at[f]], k, v, acc.at[at[f]], peak.at[f], mass.at[f])

    for f in range(2):
        for h in range(heads):
            cols = slice(h * HD, (h + 1) * HD)
            out[at[f], cols] = (acc[at[f], cols] / mass[f, h]).astype(out.dtype)


def halo_attention(info, query, acc, peak, mass, halo):
    rows, cols = query.shape
    heads = cols // HD
    f32 = jnp.float32
    stats = pltpu.VMEM((2, heads, rows // 2, 1), f32)
    return pl.pallas_call(
        halo_kernel,
        out_shape=jax.ShapeDtypeStruct((rows, cols), jnp.bfloat16),
        in_specs=[SMEM] + [VMEM] * 10,
        out_specs=VMEM,
        scratch_shapes=[pltpu.VMEM((rows, cols), f32), stats, stats],
        compiler_params=pltpu.CompilerParams(vmem_limit_bytes=32 * MIB),
        cost_estimate=pl.CostEstimate(flops=2_000_000_000, bytes_accessed=8_000_000, transcendentals=0),
        name="halo_attention",
    )(info, query, acc, peak, mass, *halo)


def on_device(
    latents, noise_level, lookback, level_table, w_query, w_key, w_value, gain_query, gain_key
):
    devices = lax.axis_size("queue")
    members = lax.axis_size("tp")
    total_cols = w_query.shape[1] * members
    core = lax.rem(lax.axis_index("queue"), 2).astype(jnp.int32)
    info = jnp.concatenate([lookback, core[None]])
    far = [(i, i + 2) for i in range(devices - 2)]
    mid = [(i, i + 1) for i in range(1, devices - 1, 2)]
    within = [(i, i + 1) for i in range(0, devices, 2)]
    back = [(i + 1, i) for i in range(0, devices, 2)]

    def move(x, pairs):
        return lax.ppermute(x, "queue", pairs)

    query, key, value, value_early, value_late, sums = project(
        noise_level, latents, level_table, w_query, w_key, w_value
    )
    far_value = move(value_early, far)
    others = [
        lax.ppermute(sums, "tp", [(i, (i + by) % members) for i in range(members)])
        for by in range(1, members)
    ]
    sums = [sums] + others
    mid_value = move(value_late, mid)
    pair_value = move(value, within)
    key_normed, key_early, key_late = normalise_key(key, gain_key[None], sums, total_cols)
    far_key = move(key_early, far)
    mid_key = move(key_late, mid)
    pair_key = move(key_normed, within)
    query_normed, acc, peak, mass = local_attention(
        info, query, gain_query[None], sums, key_normed, value, pair_key, pair_value, total_cols
    )
    near_value = move(far_value, back)
    near_key = move(far_key, back)
    return halo_attention(
        info, query_normed, acc, peak, mass,
        (far_key, far_value, mid_key, mid_value, near_key, near_value),
    )


def solution(mesh):
    in_specs = (
        P("queue", None),
        P("queue"),
        P("queue"),
        P(),
        P(None, "tp"),
        P(None, "tp"),
        P(None, "tp"),
        P("tp"),
        P("tp"),
    )
    return jax.shard_map(
        on_device, mesh=mesh, in_specs=in_specs, out_specs=P("queue", "tp"), check_vma=False
    )
```

```python
import functools

import jax
import jax.numpy as jnp
from jax import lax
from jax.experimental import pallas as pl
from jax.experimental.pallas import tpu as pltpu
from jax.sharding import PartitionSpec as P

HD = 128
WIN = 4
EPSILON = 1e-06
MIB = 2**20
EXP2_SCALE = HD ** (-0.5) * 1.4426950408889634

HBM = pl.BlockSpec(memory_space=pltpu.HBM)
VMEM = pl.BlockSpec(memory_space=pltpu.VMEM)
SMEM = pl.BlockSpec(memory_space=pltpu.SMEM)


def as_rows(column):
    wide = jnp.broadcast_to(column, (column.shape[0], 128))
    parts = [
        jnp.transpose(wide[i : i + 128])[0:1] for i in range(0, column.shape[0], 128)
    ]
    return jnp.concatenate(parts, 0)


def as_columns(rows):
    parts = [
        jnp.transpose(jnp.broadcast_to(rows[i : i + 1], (128, 128)))
        for i in range(rows.shape[0])
    ]
    return jnp.concatenate(parts, 0)


def value_kernel(
    noise_level, lookback, latents, level_table, w_query, w_key, w_value, gain_query, gain_key,
    shaped, key_weights, mixed_weights, value_both, value_early, gains_query, gains_key, info,
    levels, reaches, lat, weights, table, shift, scale, small_sem, lat_sem, w_sem,
):
    width = latents.shape[1]
    frame = latents.shape[0] // 2
    half = frame // 2
    cols = w_value.shape[1]
    main = key_weights.shape[1]
    rest = cols - main
    small = [
        pltpu.make_async_copy(src, dst, small_sem.at[i])
        for i, (src, dst) in enumerate(
            (
                (noise_level, levels),
                (level_table, table),
                (lookback, reaches),
                (gain_query, gains_query.at[0]),
                (gain_key, gains_key.at[0]),
            )
        )
    ]
    lat_copies = [
        pltpu.make_async_copy(
            latents.at[pl.ds(c * half, half)], lat.at[pl.ds(c * half, half)], lat_sem.at[c]
        )
        for c in range(4)
    ]
    for copy in small[:2] + lat_copies + small[2:]:
        copy.start()
    bounds = (0, 256, 640)
    fetches = [
        pltpu.make_async_copy(src, dst, w_sem.at[i])
        for i, (src, dst) in enumerate(
            (
                (w_value.at[:, pl.ds(0, 256)], weights.at[:, pl.ds(0, 256)]),
                (w_value.at[:, pl.ds(256, 384)], weights.at[:, pl.ds(256, 384)]),
                (w_key.at[:, pl.ds(0, main)], key_weights),
                (w_key.at[:, pl.ds(main, rest)], mixed_weights.at[:, pl.ds(0, rest)]),
                (w_query.at[:, pl.ds(0, rest)], mixed_weights.at[:, pl.ds(rest, rest)]),
            )
        )
    ]

    for copy in small[:2]:
        copy.wait()
    for f in range(2):
        chosen = lax.broadcasted_iota(jnp.int32, (table.shape[0], 1), 0) == levels[f]
        row = jnp.sum(jnp.where(chosen, table[...].astype(jnp.float32), 0.0), axis=0, keepdims=True)
        shift[f : f + 1, :] = row[:, :width]
        scale[f : f + 1, :] = 1.0 + row[:, width:]

    group = 64
    for c in range(4):
        lat_copies[c].wait()
        if c >= 1:
            fetches[c - 1].start()
        f = c // 2
        for start in range(c * half, (c + 1) * half, group):
            rows = slice(start, start + group)
            x = lat[rows, :].astype(jnp.float32)
            center = jnp.mean(x, axis=1, keepdims=True)
            x = x - center
            spread = jnp.mean(x * x, axis=1, keepdims=True)
            x = x * lax.rsqrt(spread + EPSILON)
            shaped[rows, :] = (x * scale[f : f + 1, :] + shift[f : f + 1, :]).astype(jnp.bfloat16)

    fetches[3].start()
    fetches[4].start()
    for i, (s, e) in enumerate(zip(bounds, bounds[1:])):
        fetches[i].wait()
        result = jnp.dot(shaped[...], weights[:, s:e], preferred_element_type=jnp.float32)
        turned = jnp.transpose(result).astype(jnp.bfloat16)
        value_both[s:e, :] = turned
        value_early[s:e, :] = turned[:, frame:]
    for copy in small[2:]:
        copy.wait()
    info[0] = reaches[0]
    info[1] = reaches[1]
    info[2] = lax.rem(lax.axis_index("queue"), 2)
    for copy in fetches[2:]:
        copy.wait()


def project_value(noise_level, lookback, latents, level_table, w_query, w_key, w_value, gain_query, gain_key):
    rows, width = latents.shape
    cols = w_query.shape[1]
    half = rows // 2
    main = cols // 256 * 256
    f32, bf16 = jnp.float32, jnp.bfloat16
    operands = (
        noise_level, lookback, latents, level_table, w_query, w_key, w_value, gain_query, gain_key
    )
    operands = [pltpu.with_memory_space_constraint(x, pltpu.HBM) for x in operands]
    return pl.pallas_call(
        value_kernel,
        out_shape=(
            pltpu.VMEM((rows, width), bf16),
            pltpu.VMEM((width, main), bf16),
            pltpu.VMEM((width, 2 * (cols - main)), bf16),
            pltpu.VMEM((cols, rows), bf16),
            pltpu.VMEM((cols, half), bf16),
            pltpu.VMEM((1, cols), f32),
            pltpu.VMEM((1, cols), f32),
            pltpu.SMEM((3,), jnp.int32),
        ),
        in_specs=[HBM] * 9,
        out_specs=(VMEM,) * 7 + (SMEM,),
        scratch_shapes=[
            pltpu.SMEM((2,), jnp.int32),
            pltpu.SMEM((2,), jnp.int32),
            pltpu.VMEM((rows, width), bf16),
            pltpu.VMEM((width, cols), bf16),
            pltpu.VMEM(level_table.shape, bf16),
            pltpu.VMEM((2, width), f32),
            pltpu.VMEM((2, width), f32),
            pltpu.SemaphoreType.DMA((5,)),
            pltpu.SemaphoreType.DMA((4,)),
            pltpu.SemaphoreType.DMA((5,)),
        ],
        compiler_params=pltpu.CompilerParams(vmem_limit_bytes=18 * MIB),
        cost_estimate=pl.CostEstimate(
            flops=2 * rows * width * cols, bytes_accessed=26_000_000, transcendentals=0
        ),
        name="project_value",
    )(*operands)


def query_key_kernel(shaped, key_weights, mixed_weights, w_query, query, key, sums_out, weights, sem):
    cols = query.shape[1]
    main = key_weights.shape[1]
    rest = cols - main
    fetch = pltpu.make_async_copy(w_query.at[:, pl.ds(rest, main)], weights, sem.at[0])
    fetch.start()

    def dot(w):
        return jnp.dot(shaped[...], w[...], preferred_element_type=jnp.float32)

    key[:, :main] = dot(key_weights)
    middle = dot(mixed_weights)
    key[:, main:] = middle[:, :rest]
    query[:, :rest] = middle[:, rest:]
    fetch.wait()
    query[:, rest:] = dot(weights)
    for at, ref in ((0, key), (4, query)):
        x = ref[...]
        sums_out[at : at + 4, :] = as_rows(jnp.sum(x * x, axis=1, keepdims=True))


def project_query_key(shaped, key_weights, mixed_weights, w_query):
    rows, width = shaped.shape
    cols = w_query.shape[1]
    f32 = jnp.float32
    return pl.pallas_call(
        query_key_kernel,
        out_shape=(
            pltpu.VMEM((rows, cols), f32),
            pltpu.VMEM((rows, cols), f32),
            pltpu.VMEM((8, 128), f32),
        ),
        in_specs=[VMEM] * 3 + [HBM],
        out_specs=(VMEM,) * 3,
        scratch_shapes=[pltpu.VMEM(key_weights.shape, jnp.bfloat16), pltpu.SemaphoreType.DMA((1,))],
        compiler_params=pltpu.CompilerParams(vmem_limit_bytes=16 * MIB),
        cost_estimate=pl.CostEstimate(
            flops=4 * rows * width * cols, bytes_accessed=18_000_000, transcendentals=0
        ),
        name="project_query_key",
    )(shaped, key_weights, mixed_weights, pltpu.with_memory_space_constraint(w_query, pltpu.HBM))


def norm_factor(sums, at, total_cols):
    first, second, third, fourth = (x[at : at + 4, :] for x in sums)
    return as_columns(lax.rsqrt((first + second + (third + fourth)) / total_cols + EPSILON))


def key_kernel(total_cols, key, gain, s0, s1, s2, s3, all_out, early, late):
    factor = norm_factor((s0, s1, s2, s3), 0, total_cols)
    half = late.shape[0]
    for c in range(0, key.shape[1], 128):
        normed = (key[:, c : c + 128] * factor * gain[0:1, c : c + 128]).astype(jnp.bfloat16)
        all_out[:, c : c + 128] = normed
        late[:, c : c + 128] = normed[:half]
        early[:, c : c + 128] = normed[half:]


def normalise_key(key, gain, sums, total_cols):
    rows, cols = key.shape
    bf16 = jnp.bfloat16
    return pl.pallas_call(
        functools.partial(key_kernel, total_cols),
        out_shape=(
            jax.ShapeDtypeStruct((rows, cols), bf16),
            jax.ShapeDtypeStruct((rows // 2, cols), bf16),
            jax.ShapeDtypeStruct((rows // 2, cols), bf16),
        ),
        in_specs=[VMEM] * 6,
        out_specs=(VMEM,) * 3,
        compiler_params=pltpu.CompilerParams(vmem_limit_bytes=12 * MIB),
        cost_estimate=pl.CostEstimate(flops=2 * rows * cols, bytes_accessed=100_000, transcendentals=0),
        name="normalise_key",
    )(key, gain, *sums)


def attend_block(first, q, k, vt, acc, peak, mass):
    heads = q.shape[1] // HD
    cols = [slice(h * HD, (h + 1) * HD) for h in range(heads)]
    scores = [
        lax.dot_general(k[:, c], q[:, c], (((1,), (1,)), ((), ())), preferred_element_type=jnp.float32)
        for c in cols
    ]
    tops = [jnp.max(s, axis=0, keepdims=True) for s in scores]
    if not first:
        olds = [peak[h : h + 1, :] for h in range(heads)]
        tops = [jnp.maximum(t, o) for t, o in zip(tops, olds)]
        fades = [jnp.exp2((o - t) * EXP2_SCALE) for t, o in zip(tops, olds)]
    expos = [jnp.exp2((s - t) * EXP2_SCALE) for s, t in zip(scores, tops)]
    for h in range(heads):
        total = jnp.sum(expos[h], axis=0, keepdims=True)
        peak[h : h + 1, :] = tops[h]
        mass[h : h + 1, :] = total if first else mass[h : h + 1, :] * fades[h] + total
    for h, c in enumerate(cols):
        part = jnp.dot(vt[c, :], expos[h].astype(jnp.bfloat16), preferred_element_type=jnp.float32)
        acc[c, :] = part if first else acc[c, :] * fades[h] + part


def local_kernel(
    total_cols, info, query, gain, s0, s1, s2, s3, key, value, pair_key_0, pair_key_1, pair_value,
    query_out, acc, peak, mass,
):
    factor = norm_factor((s0, s1, s2, s3), 4, total_cols)
    for c in range(0, query.shape[1], 128):
        query_out[:, c : c + 128] = (
            query[:, c : c + 128] * factor * gain[0:1, c : c + 128]
        ).astype(jnp.bfloat16)
    frame = query.shape[0] // 2
    at = [pl.ds(0, frame), pl.ds(frame, frame)]
    for f in range(2):
        parts = (acc.at[f], peak.at[f], mass.at[f])
        q = query_out.at[at[f]]
        attend_block(True, q, key.at[at[f]], value.at[:, at[f]], *parts)
        if f == 1:

            @pl.when(info[f] >= 1)
            def _():
                attend_block(False, q, key.at[at[0]], value.at[:, at[0]], *parts)

        for g, k in ((0, pair_key_0), (1, pair_key_1)):

            @pl.when(jnp.logical_and(info[2] == 1, info[f] >= f + 2 - g))
            def _():
                attend_block(False, q, k, pair_value.at[:, at[g]], *parts)


def local_attention(info, query, gain, sums, key, value, pairs, total_cols):
    rows, cols = query.shape
    f32 = jnp.float32
    stats = jax.ShapeDtypeStruct((2, 8, rows // 2), f32)
    return pl.pallas_call(
        functools.partial(local_kernel, total_cols),
        out_shape=(
            jax.ShapeDtypeStruct((rows, cols), jnp.bfloat16),
            jax.ShapeDtypeStruct((2, cols, rows // 2), f32),
            stats,
            stats,
        ),
        in_specs=[SMEM] + [VMEM] * 11,
        out_specs=(VMEM,) * 4,
        compiler_params=pltpu.CompilerParams(vmem_limit_bytes=12 * MIB),
        cost_estimate=pl.CostEstimate(flops=3_000_000, bytes_accessed=100_000, transcendentals=0),
        name="local_attention",
    )(info, query, gain, *sums, key, value, *pairs)


def near_kernel(info, query, acc_in, peak_in, mass_in, mid_keys, near_keys, values, acc, peak, mass):
    keys = (mid_keys, near_keys)
    frame = query.shape[0] // 2
    at = [pl.ds(0, frame), pl.ds(frame, frame)]
    acc[...] = acc_in[...]
    peak[...] = peak_in[...]
    mass[...] = mass_in[...]
    for f, reach, g in ((0, 1, 1), (0, 2, 0), (1, 2, 1), (1, 3, 0)):

        @pl.when(jnp.logical_and(info[2] == 0, info[f] >= reach))
        def _():
            attend_block(
                False, query.at[at[f]], keys[g], values.at[:, at[g]],
                acc.at[f], peak.at[f], mass.at[f],
            )


def near_attention(info, query, acc, peak, mass, mid_keys, near_keys, values):
    rows, cols = query.shape
    f32 = jnp.float32
    stats = jax.ShapeDtypeStruct((2, 8, rows // 2), f32)
    return pl.pallas_call(
        near_kernel,
        out_shape=(jax.ShapeDtypeStruct((2, cols, rows // 2), f32), stats, stats),
        in_specs=[SMEM] + [VMEM] * 7,
        out_specs=(VMEM,) * 3,
        compiler_params=pltpu.CompilerParams(vmem_limit_bytes=12 * MIB),
        cost_estimate=pl.CostEstimate(flops=1_000_000, bytes_accessed=100_000, transcendentals=0),
        name="near_attention",
    )(info, query, acc, peak, mass, mid_keys, near_keys, values)


def far_kernel(
    info, query, acc_in, peak_in, mass_in, far_keys, far_values, relayed_keys, relayed_values,
    out, acc, peak, mass,
):
    cols = query.shape[1]
    frame = query.shape[0] // 2
    at = [pl.ds(0, frame), pl.ds(frame, frame)]
    acc[...] = acc_in[0]
    peak[...] = peak_in[0]
    mass[...] = mass_in[0]
    for core, k, v in (
        (0, far_keys, far_values),
        (1, relayed_keys, relayed_values.at[:, at[1]]),
    ):

        @pl.when(jnp.logical_and(info[2] == core, info[0] >= 3))
        def _():
            attend_block(False, query.at[at[0]], k, v, acc, peak, mass)

    for f in range(2):
        for h in range(cols // HD):
            c = slice(h * HD, (h + 1) * HD)
            if f == 0:
                result = acc[c, :] / mass[h : h + 1, :]
            else:
                result = acc_in[f, c, :] / mass_in[f, h : h + 1, :]
            out[at[f], c] = jnp.transpose(result).astype(out.dtype)


def far_attention(info, query, acc, peak, mass, halo):
    rows, cols = query.shape
    f32 = jnp.float32
    stats = pltpu.VMEM((8, rows // 2), f32)
    return pl.pallas_call(
        far_kernel,
        out_shape=jax.ShapeDtypeStruct((rows, cols), jnp.bfloat16),
        in_specs=[SMEM] + [VMEM] * 8,
        out_specs=VMEM,
        scratch_shapes=[pltpu.VMEM((cols, rows // 2), f32), stats, stats],
        compiler_params=pltpu.CompilerParams(vmem_limit_bytes=12 * MIB),
        cost_estimate=pl.CostEstimate(flops=1_000_000, bytes_accessed=100_000, transcendentals=0),
        name="far_attention",
    )(info, query, acc, peak, mass, *halo)


def on_device(
    latents, noise_level, lookback, level_table, w_query, w_key, w_value, gain_query, gain_key
):
    devices = lax.axis_size("queue")
    total_cols = w_query.shape[1] * lax.axis_size("tp")
    along = [(i, (i + 1) % devices) for i in range(devices)]
    swap = [(i, i ^ 1) for i in range(devices)]

    def move(x, pairs):
        return lax.ppermute(x, "queue", pairs)

    shaped, key_weights, mixed_weights, value, value_early, gain_query, gain_key, info = project_value(
        noise_level, lookback, latents, level_table, w_query, w_key, w_value,
        gain_query, gain_key,
    )
    info = pltpu.with_memory_space_constraint(info, pltpu.SMEM)
    near_value = move(value, along)
    far_value = move(move(value_early, swap), along)
    query, key, sums = project_query_key(shaped, key_weights, mixed_weights, w_query)
    sums = [sums] + [
        lax.ppermute(sums, "tp", pairs)
        for pairs in (
            [(0, 1), (1, 0), (2, 3), (3, 2)],
            [(0, 3), (3, 0), (1, 2), (2, 1)],
            [(0, 2), (2, 0), (1, 3), (3, 1)],
        )
    ]
    key_normed, key_early, key_late = normalise_key(key, gain_key, sums, total_cols)
    key_normed, far_value, near_value = lax.optimization_barrier((key_normed, far_value, near_value))
    relayed_value = move(near_value, swap)
    near_key = move(key_early, along)
    mid_key = move(key_late, along)
    pair_key_1 = move(key_early, swap)
    pair_key_0 = move(key_late, swap)
    far_key = move(pair_key_1, along)
    query_normed, acc, peak, mass = local_attention(
        info, query, gain_query, sums, key_normed, value, (pair_key_0, pair_key_1, near_value), total_cols
    )
    near_key, acc = lax.optimization_barrier((near_key, acc))
    relayed_key = move(near_key, swap)
    acc, peak, mass = near_attention(info, query_normed, acc, peak, mass, mid_key, near_key, near_value)
    return far_attention(
        info, query_normed, acc, peak, mass, (far_key, far_value, relayed_key, relayed_value)
    )


def solution(mesh):
    in_specs = (
        P("queue", None),
        P("queue"),
        P("queue"),
        P(),
        P(None, "tp"),
        P(None, "tp"),
        P(None, "tp"),
        P("tp"),
        P("tp"),
    )
    return jax.shard_map(
        on_device, mesh=mesh, in_specs=in_specs, out_specs=P("queue", "tp"), check_vma=False
    )
```

```python
import functools

import jax
import jax.numpy as jnp
from jax import lax
from jax.experimental import pallas as pl
from jax.experimental.pallas import tpu as pltpu
from jax.sharding import PartitionSpec as P

HD = 128
WIN = 4
EPSILON = 1e-06
MIB = 2**20
PADDING = 16
EXP2_SCALE = HD ** (-0.5) * 1.4426950408889634

HBM = pl.BlockSpec(memory_space=pltpu.HBM)
VMEM = pl.BlockSpec(memory_space=pltpu.VMEM)
SMEM = pl.BlockSpec(memory_space=pltpu.SMEM)


def as_rows(column):
    wide = jnp.broadcast_to(column, (column.shape[0], 128))
    parts = [
        jnp.transpose(wide[i : i + 128])[0:1] for i in range(0, column.shape[0], 128)
    ]
    return jnp.concatenate(parts, 0)


def as_columns(rows):
    parts = [
        jnp.transpose(jnp.broadcast_to(rows[i : i + 1], (128, 128)))
        for i in range(rows.shape[0])
    ]
    return jnp.concatenate(parts, 0)


def value_kernel(
    noise_level, lookback, latents, level_table, w_query, w_key, w_value, gain_query, gain_key,
    shaped, key_weights, mixed_weights, value_both, value_early, gains_query, gains_key, info,
    levels, reaches, lat, weights, table, shift, scale, small_sem, lat_sem, w_sem,
):
    width = latents.shape[1]
    frame = latents.shape[0] // 2
    half = frame // 2
    cols = w_value.shape[1]
    main = key_weights.shape[1]
    rest = cols - main
    small = [
        pltpu.make_async_copy(src, dst, small_sem.at[i])
        for i, (src, dst) in enumerate(
            (
                (noise_level, levels),
                (level_table, table),
                (lookback, reaches),
                (gain_query, gains_query.at[0]),
                (gain_key, gains_key.at[0]),
            )
        )
    ]
    lat_copies = [
        pltpu.make_async_copy(
            latents.at[pl.ds(c * half, half)], lat.at[pl.ds(c * half, half)], lat_sem.at[c]
        )
        for c in range(4)
    ]
    for copy in lat_copies[:1] + small[:2] + lat_copies[1:] + small[2:]:
        copy.start()
    fetches = [
        pltpu.make_async_copy(src, dst, w_sem.at[i])
        for i, (src, dst) in enumerate(
            (
                (w_value.at[:, pl.ds(0, 256)], weights.at[:, pl.ds(0, 256)]),
                (w_value.at[:, pl.ds(256, 384)], weights.at[:, pl.ds(256, 384)]),
                (w_key.at[:, pl.ds(0, main)], key_weights),
                (w_key.at[:, pl.ds(main, rest)], mixed_weights.at[:, pl.ds(0, rest)]),
                (w_query.at[:, pl.ds(0, rest)], mixed_weights.at[:, pl.ds(rest, rest)]),
            )
        )
    ]

    for copy in small[:2]:
        copy.wait()
    pick = lax.broadcasted_iota(jnp.int32, (8, 1), 0)
    wanted = jnp.where(pick == 0, levels[0], levels[1])
    chosen = lax.broadcasted_iota(jnp.int32, (8, table.shape[0]), 1) == wanted
    rows = jnp.dot(
        chosen.astype(jnp.float32).astype(jnp.bfloat16), table[...], preferred_element_type=jnp.float32
    )
    shift[...] = rows[0:2, :width]
    scale[...] = 1.0 + rows[0:2, width:]

    def shape_rows(f, start, count):
        rows = slice(start, start + count)
        x = lat[rows, :].astype(jnp.float32)
        center = jnp.mean(x, axis=1, keepdims=True)
        x = x - center
        spread = jnp.mean(x * x, axis=1, keepdims=True)
        x = x * lax.rsqrt(spread + EPSILON)
        shaped[rows, :] = (x * scale[f : f + 1, :] + shift[f : f + 1, :]).astype(jnp.bfloat16)

    def value_rows(f):
        rows = slice(f * frame, (f + 1) * frame)
        result = jnp.dot(shaped[rows, :], weights[...], preferred_element_type=jnp.float32)
        turned = jnp.transpose(result).astype(jnp.bfloat16)
        value_both[:, rows] = turned
        if f == 1:
            value_early[...] = turned

    group = 64
    for c in range(2):
        lat_copies[c].wait()
        fetches[c].start()
        for j in range(c * half, (c + 1) * half, group):
            shape_rows(0, j, group)
    for c in range(2, 4):
        lat_copies[c].wait()
        fetches[c].start()
    fetches[4].start()
    fetches[0].wait()
    fetches[1].wait()
    for j in range(frame, 2 * frame, group):
        shape_rows(1, j, group)
    value_rows(0)
    value_rows(1)
    for copy in small[2:]:
        copy.wait()
    info[0] = reaches[0]
    info[1] = reaches[1]
    info[2] = lax.rem(lax.axis_index("queue"), 2)
    for copy in fetches[2:]:
        copy.wait()


def project_value(noise_level, lookback, latents, level_table, w_query, w_key, w_value, gain_query, gain_key):
    rows, width = latents.shape
    cols = w_query.shape[1]
    half = rows // 2
    main = cols // 256 * 256
    f32, bf16 = jnp.float32, jnp.bfloat16
    operands = (
        noise_level, lookback, latents, level_table, w_query, w_key, w_value, gain_query, gain_key
    )
    operands = [pltpu.with_memory_space_constraint(x, pltpu.HBM) for x in operands]
    return pl.pallas_call(
        value_kernel,
        out_shape=(
            pltpu.VMEM((rows, width), bf16),
            pltpu.VMEM((width, main), bf16),
            pltpu.VMEM((width, 2 * (cols - main)), bf16),
            pltpu.VMEM((cols, rows), bf16),
            pltpu.VMEM((cols, half), bf16),
            pltpu.VMEM((1, cols), f32),
            pltpu.VMEM((1, cols), f32),
            pltpu.SMEM((3,), jnp.int32),
        ),
        in_specs=[HBM] * 9,
        out_specs=(VMEM,) * 7 + (SMEM,),
        scratch_shapes=[
            pltpu.SMEM((2,), jnp.int32),
            pltpu.SMEM((2,), jnp.int32),
            pltpu.VMEM((rows, width), bf16),
            pltpu.VMEM((width, cols), bf16),
            pltpu.VMEM(level_table.shape, bf16),
            pltpu.VMEM((2, width), f32),
            pltpu.VMEM((2, width), f32),
            pltpu.SemaphoreType.DMA((5,)),
            pltpu.SemaphoreType.DMA((4,)),
            pltpu.SemaphoreType.DMA((5,)),
        ],
        compiler_params=pltpu.CompilerParams(vmem_limit_bytes=22 * MIB),
        cost_estimate=pl.CostEstimate(
            flops=2 * rows * width * cols, bytes_accessed=26_000_000, transcendentals=0
        ),
        name="project_value",
    )(*operands)


def query_key_kernel(shaped, key_weights, mixed_weights, w_query, query, key, sums_out, weights, sem):
    cols = query.shape[1]
    main = key_weights.shape[1]
    rest = cols - main
    fetch = pltpu.make_async_copy(w_query.at[:, pl.ds(rest, main)], weights, sem.at[0])
    fetch.start()

    def dot(w):
        return jnp.dot(shaped[...], w[...], preferred_element_type=jnp.float32)

    key[:, :main] = dot(key_weights)
    middle = dot(mixed_weights)
    key[:, main:] = middle[:, :rest]
    query[:, :rest] = middle[:, rest:]
    fetch.wait()
    query[:, rest:] = dot(weights)
    for at, ref in ((0, key), (4, query)):
        x = ref[...]
        sums_out[at : at + 4, :] = as_rows(jnp.sum(x * x, axis=1, keepdims=True))


def project_query_key(shaped, key_weights, mixed_weights, w_query):
    rows, width = shaped.shape
    cols = w_query.shape[1]
    f32 = jnp.float32
    return pl.pallas_call(
        query_key_kernel,
        out_shape=(
            pltpu.VMEM((rows, cols), f32),
            pltpu.VMEM((rows, cols), f32),
            pltpu.VMEM((8, 128), f32),
        ),
        in_specs=[VMEM] * 3 + [HBM],
        out_specs=(VMEM,) * 3,
        scratch_shapes=[pltpu.VMEM(key_weights.shape, jnp.bfloat16), pltpu.SemaphoreType.DMA((1,))],
        compiler_params=pltpu.CompilerParams(vmem_limit_bytes=16 * MIB),
        cost_estimate=pl.CostEstimate(
            flops=4 * rows * width * cols, bytes_accessed=18_000_000, transcendentals=0
        ),
        name="project_query_key",
    )(shaped, key_weights, mixed_weights, pltpu.with_memory_space_constraint(w_query, pltpu.HBM))


def norm_factor(sums, at, total_cols):
    first, second, third, fourth = (x[at : at + 4, :] for x in sums)
    return as_columns(lax.rsqrt((first + second + (third + fourth)) / total_cols + EPSILON))


def key_kernel(total_cols, key, gain, s0, s1, s2, s3, all_out, early, late, passed):
    factor = norm_factor((s0, s1, s2, s3), 0, total_cols)
    half = early.shape[0]
    for c in range(0, key.shape[1], 128):
        normed = (key[:, c : c + 128] * factor * gain[0:1, c : c + 128]).astype(jnp.bfloat16)
        all_out[:, c : c + 128] = normed
        late[:half, c : c + 128] = normed[:half]
        late[half:, c : c + 128] = normed[: 2 * PADDING]
        early[:, c : c + 128] = normed[half:]
        passed[:half, c : c + 128] = normed[half:]
        passed[half:, c : c + 128] = normed[-PADDING:]


def normalise_key(key, gain, sums, total_cols):
    rows, cols = key.shape
    bf16 = jnp.bfloat16
    return pl.pallas_call(
        functools.partial(key_kernel, total_cols),
        out_shape=(
            jax.ShapeDtypeStruct((rows, cols), bf16),
            jax.ShapeDtypeStruct((rows // 2, cols), bf16),
            jax.ShapeDtypeStruct((rows // 2 + 2 * PADDING, cols), bf16),
            jax.ShapeDtypeStruct((rows // 2 + PADDING, cols), bf16),
        ),
        in_specs=[VMEM] * 6,
        out_specs=(VMEM,) * 4,
        compiler_params=pltpu.CompilerParams(vmem_limit_bytes=12 * MIB),
        cost_estimate=pl.CostEstimate(flops=2 * rows * cols, bytes_accessed=100_000, transcendentals=0),
        name="normalise_key",
    )(key, gain, *sums)


def attend_block(first, q, k, vt, acc, peak, mass):
    heads = q.shape[1] // HD
    cols = [slice(h * HD, (h + 1) * HD) for h in range(heads)]
    scores = [
        lax.dot_general(k[:, c], q[:, c], (((1,), (1,)), ((), ())), preferred_element_type=jnp.float32)
        for c in cols
    ]
    tops = [jnp.max(s, axis=0, keepdims=True) for s in scores]
    if not first:
        olds = [peak[h : h + 1, :] for h in range(heads)]
        tops = [jnp.maximum(t, o) for t, o in zip(tops, olds)]
        fades = [jnp.exp2((o - t) * EXP2_SCALE) for t, o in zip(tops, olds)]
    expos = [jnp.exp2((s - t) * EXP2_SCALE) for s, t in zip(scores, tops)]
    for h in range(heads):
        total = jnp.sum(expos[h], axis=0, keepdims=True)
        peak[h : h + 1, :] = tops[h]
        mass[h : h + 1, :] = total if first else mass[h : h + 1, :] * fades[h] + total
    for h, c in enumerate(cols):
        part = jnp.dot(vt[c, :], expos[h].astype(jnp.bfloat16), preferred_element_type=jnp.float32)
        acc[c, :] = part if first else acc[c, :] * fades[h] + part


def local_kernel(
    total_cols, info, query, gain, s0, s1, s2, s3, key, value, query_out, acc, peak, mass,
):
    factor = norm_factor((s0, s1, s2, s3), 4, total_cols)
    for c in range(0, query.shape[1], 128):
        query_out[:, c : c + 128] = (
            query[:, c : c + 128] * factor * gain[0:1, c : c + 128]
        ).astype(jnp.bfloat16)
    frame = query.shape[0] // 2
    at = [pl.ds(0, frame), pl.ds(frame, frame)]
    for f in range(2):
        attend_block(
            True, query_out.at[at[f]], key.at[at[f]], value.at[:, at[f]],
            acc.at[f], peak.at[f], mass.at[f],
        )

    @pl.when(info[1] >= 1)
    def _():
        attend_block(
            False, query_out.at[at[1]], key.at[at[0]], value.at[:, at[0]],
            acc.at[1], peak.at[1], mass.at[1],
        )


def local_attention(info, query, gain, sums, key, value, total_cols):
    rows, cols = query.shape
    f32 = jnp.float32
    return pl.pallas_call(
        functools.partial(local_kernel, total_cols),
        out_shape=(
            pltpu.VMEM((rows, cols), jnp.bfloat16),
            pltpu.VMEM((2, cols, rows // 2), f32),
            pltpu.VMEM((2, 8, rows // 2), f32),
            pltpu.VMEM((2, 8, rows // 2), f32),
        ),
        in_specs=[SMEM] + [VMEM] * 8,
        out_specs=(VMEM,) * 4,
        compiler_params=pltpu.CompilerParams(vmem_limit_bytes=12 * MIB),
        cost_estimate=pl.CostEstimate(flops=3_000_000, bytes_accessed=100_000, transcendentals=0),
        name="local_attention",
    )(info, query, gain, *sums, key, value)


def near_kernel(info, query, acc_in, peak_in, mass_in, mid_keys, near_keys, values, acc, peak, mass):
    frame = query.shape[0] // 2
    keys = (mid_keys.at[pl.ds(0, frame)], near_keys)
    at = [pl.ds(0, frame), pl.ds(frame, frame)]
    acc[...] = acc_in[...]
    peak[...] = peak_in[...]
    mass[...] = mass_in[...]
    for f, reach, g in ((0, 1, 1), (0, 2, 0), (1, 2, 1), (1, 3, 0)):

        @pl.when(info[f] >= reach)
        def _():
            attend_block(
                False, query.at[at[f]], keys[g], values.at[:, at[g]],
                acc.at[f], peak.at[f], mass.at[f],
            )


def near_attention(info, query, acc, peak, mass, mid_keys, near_keys, values):
    rows, cols = query.shape
    f32 = jnp.float32
    stats = jax.ShapeDtypeStruct((2, 8, rows // 2), f32)
    return pl.pallas_call(
        near_kernel,
        out_shape=(jax.ShapeDtypeStruct((2, cols, rows // 2), f32), stats, stats),
        in_specs=[SMEM] + [VMEM] * 7,
        out_specs=(VMEM,) * 3,
        compiler_params=pltpu.CompilerParams(vmem_limit_bytes=12 * MIB),
        cost_estimate=pl.CostEstimate(flops=1_000_000, bytes_accessed=100_000, transcendentals=0),
        name="near_attention",
    )(info, query, acc, peak, mass, mid_keys, near_keys, values)


def far_kernel(
    info, query, acc_in, peak_in, mass_in, far_keys, far_values, relayed_keys, relayed_values,
    out, acc, peak, mass,
):
    cols = query.shape[1]
    frame = query.shape[0] // 2
    at = [pl.ds(0, frame), pl.ds(frame, frame)]
    acc[...] = acc_in[0]
    peak[...] = peak_in[0]
    mass[...] = mass_in[0]
    for core, k, v in (
        (0, far_keys.at[at[0]], far_values),
        (1, relayed_keys, relayed_values.at[:, at[1]]),
    ):

        @pl.when(jnp.logical_and(info[2] == core, info[0] >= 3))
        def _():
            attend_block(False, query.at[at[0]], k, v, acc, peak, mass)

    for f in range(2):
        for h in range(cols // HD):
            c = slice(h * HD, (h + 1) * HD)
            if f == 0:
                result = acc[c, :] / mass[h : h + 1, :]
            else:
                result = acc_in[f, c, :] / mass_in[f, h : h + 1, :]
            out[at[f], c] = jnp.transpose(result).astype(out.dtype)


def far_attention(info, query, acc, peak, mass, halo):
    rows, cols = query.shape
    f32 = jnp.float32
    stats = pltpu.VMEM((8, rows // 2), f32)
    return pl.pallas_call(
        far_kernel,
        out_shape=jax.ShapeDtypeStruct((rows, cols), jnp.bfloat16),
        in_specs=[SMEM] + [VMEM] * 8,
        out_specs=VMEM,
        scratch_shapes=[pltpu.VMEM((cols, rows // 2), f32), stats, stats],
        compiler_params=pltpu.CompilerParams(vmem_limit_bytes=12 * MIB),
        cost_estimate=pl.CostEstimate(flops=1_000_000, bytes_accessed=100_000, transcendentals=0),
        name="far_attention",
    )(info, query, acc, peak, mass, *halo)


def on_device(
    latents, noise_level, lookback, level_table, w_query, w_key, w_value, gain_query, gain_key
):
    devices = lax.axis_size("queue")
    members = lax.axis_size("tp")
    total_cols = w_query.shape[1] * members
    along = [(i, (i + 1) % devices) for i in range(devices)]
    swap = [(i, i ^ 1) for i in range(devices)]

    def facing(i, t):
        if i in (0, devices - 1):
            return i * members + (t ^ 1)
        return (i + 1 if i % 2 else i - 1) * members + t

    across = [(i * members + t, facing(i, t)) for i in range(devices) for t in range(members)]

    def move(x, pairs):
        return lax.ppermute(x, "queue", pairs)

    def move_across(x):
        return lax.ppermute(x, ("queue", "tp"), across)

    shaped, key_weights, mixed_weights, value, value_early, gain_query, gain_key, info = project_value(
        noise_level, lookback, latents, level_table, w_query, w_key, w_value, gain_query, gain_key
    )
    info = pltpu.with_memory_space_constraint(info, pltpu.SMEM)
    near_value = move(value, along)
    pair_value = move(value_early, swap)
    query, key, sums = project_query_key(shaped, key_weights, mixed_weights, w_query)
    pair_value, sums = lax.optimization_barrier((pair_value, sums))
    sums = [sums] + [
        lax.ppermute(sums, "tp", pairs)
        for pairs in (
            [(0, 1), (1, 0), (2, 3), (3, 2)],
            [(0, 3), (3, 0), (1, 2), (2, 1)],
            [(0, 2), (2, 0), (1, 3), (3, 1)],
        )
    ]
    far_value = move(pair_value, along)
    key_normed, key_early, key_late, key_passed = normalise_key(key, gain_key, sums, total_cols)
    key_normed, far_value, near_value = lax.optimization_barrier((key_normed, far_value, near_value))
    relayed_value = move(near_value, swap)
    near_key = move(key_early, along)
    mid_key = move(key_late, along)
    pair_key = move(key_passed, swap)
    far_key = move_across(pair_key)
    key_normed, pair_key = lax.optimization_barrier((key_normed, pair_key))
    query_normed, acc, peak, mass = local_attention(
        info, query, gain_query, sums, key_normed, value, total_cols
    )
    near_key, acc = lax.optimization_barrier((near_key, acc))
    relayed_key = move(near_key, swap)
    acc, peak, mass = near_attention(info, query_normed, acc, peak, mass, mid_key, near_key, near_value)
    return far_attention(
        info, query_normed, acc, peak, mass, (far_key, far_value, relayed_key, relayed_value)
    )


def solution(mesh):
    in_specs = (
        P("queue", None),
        P("queue"),
        P("queue"),
        P(),
        P(None, "tp"),
        P(None, "tp"),
        P(None, "tp"),
        P("tp"),
        P("tp"),
    )
    return jax.shard_map(
        on_device, mesh=mesh, in_specs=in_specs, out_specs=P("queue", "tp"), check_vma=False
    )
```

```python
import functools

import jax
import jax.numpy as jnp
from jax import lax
from jax.experimental import pallas as pl
from jax.experimental.pallas import tpu as pltpu
from jax.sharding import PartitionSpec as P

HD = 128
WIN = 4
EPSILON = 1e-06
MIB = 2**20
VALUE_PADDING = 80
PADDING = 16
EXP2_SCALE = HD ** (-0.5) * 1.4426950408889634

HBM = pl.BlockSpec(memory_space=pltpu.HBM)
VMEM = pl.BlockSpec(memory_space=pltpu.VMEM)
SMEM = pl.BlockSpec(memory_space=pltpu.SMEM)


def as_rows(column):
    wide = jnp.broadcast_to(column, (column.shape[0], 128))
    parts = [
        jnp.transpose(wide[i : i + 128])[0:1] for i in range(0, column.shape[0], 128)
    ]
    return jnp.concatenate(parts, 0)


def as_columns(rows):
    parts = [
        jnp.transpose(jnp.broadcast_to(rows[i : i + 1], (128, 128)))
        for i in range(rows.shape[0])
    ]
    return jnp.concatenate(parts, 0)


def value_kernel(
    noise_level, lookback, latents, level_table, w_query, w_key, w_value, gain_query, gain_key,
    shaped, key_weights, mixed_weights, value_both, value_early, gains_query, gains_key, info,
    levels, reaches, lat, weights, table, shift, scale, small_sem, lat_sem, w_sem,
):
    width = latents.shape[1]
    frame = latents.shape[0] // 2
    half = frame // 2
    cols = w_value.shape[1]
    main = key_weights.shape[1]
    rest = cols - main
    small = [
        pltpu.make_async_copy(src, dst, small_sem.at[i])
        for i, (src, dst) in enumerate(
            (
                (noise_level, levels),
                (level_table, table),
                (lookback, reaches),
                (gain_query, gains_query.at[0]),
                (gain_key, gains_key.at[0]),
            )
        )
    ]
    lat_copies = [
        pltpu.make_async_copy(
            latents.at[pl.ds(c * half, half)], lat.at[pl.ds(c * half, half)], lat_sem.at[c]
        )
        for c in range(4)
    ]
    for copy in lat_copies[:1] + small[:2] + lat_copies[1:] + small[2:]:
        copy.start()
    fetches = [
        pltpu.make_async_copy(src, dst, w_sem.at[i])
        for i, (src, dst) in enumerate(
            (
                (w_value.at[:, pl.ds(0, 256)], weights.at[:, pl.ds(0, 256)]),
                (w_value.at[:, pl.ds(256, 384)], weights.at[:, pl.ds(256, 384)]),
                (w_key.at[:, pl.ds(0, main)], key_weights),
                (w_key.at[:, pl.ds(main, rest)], mixed_weights.at[:, pl.ds(0, rest)]),
                (w_query.at[:, pl.ds(0, rest)], mixed_weights.at[:, pl.ds(rest, rest)]),
            )
        )
    ]

    for copy in small[:2]:
        copy.wait()
    pick = lax.broadcasted_iota(jnp.int32, (8, 1), 0)
    wanted = jnp.where(pick == 0, levels[0], levels[1])
    chosen = lax.broadcasted_iota(jnp.int32, (8, table.shape[0]), 1) == wanted
    rows = jnp.dot(
        chosen.astype(jnp.float32).astype(jnp.bfloat16), table[...], preferred_element_type=jnp.float32
    )
    shift[...] = rows[0:2, :width]
    scale[...] = 1.0 + rows[0:2, width:]

    def shape_rows(f, start, count):
        rows = slice(start, start + count)
        x = lat[rows, :].astype(jnp.float32)
        center = jnp.mean(x, axis=1, keepdims=True)
        x = x - center
        spread = jnp.mean(x * x, axis=1, keepdims=True)
        x = x * lax.rsqrt(spread + EPSILON)
        shaped[rows, :] = (x * scale[f : f + 1, :] + shift[f : f + 1, :]).astype(jnp.bfloat16)

    def value_rows(f):
        rows = slice(f * frame, (f + 1) * frame)
        result = jnp.dot(shaped[rows, :], weights[...], preferred_element_type=jnp.float32)
        turned = jnp.transpose(result).astype(jnp.bfloat16)
        value_both[:, rows] = turned
        if f == 1:
            value_early[:cols, :] = turned
            value_early[cols:, :] = turned[:VALUE_PADDING]

    group = 64
    for c in range(2):
        lat_copies[c].wait()
        fetches[c].start()
        for j in range(c * half, (c + 1) * half, group):
            shape_rows(0, j, group)
    for c in range(2, 4):
        lat_copies[c].wait()
        fetches[c].start()
    fetches[4].start()
    fetches[0].wait()
    fetches[1].wait()
    for j in range(frame, 2 * frame, group):
        shape_rows(1, j, group)
    value_rows(0)
    value_rows(1)
    for copy in small[2:]:
        copy.wait()
    info[0] = reaches[0]
    info[1] = reaches[1]
    info[2] = lax.rem(lax.axis_index("queue"), 2)
    for copy in fetches[2:]:
        copy.wait()


def project_value(noise_level, lookback, latents, level_table, w_query, w_key, w_value, gain_query, gain_key):
    rows, width = latents.shape
    cols = w_query.shape[1]
    half = rows // 2
    main = cols // 256 * 256
    f32, bf16 = jnp.float32, jnp.bfloat16
    operands = (
        noise_level, lookback, latents, level_table, w_query, w_key, w_value, gain_query, gain_key
    )
    operands = [pltpu.with_memory_space_constraint(x, pltpu.HBM) for x in operands]
    return pl.pallas_call(
        value_kernel,
        out_shape=(
            pltpu.VMEM((rows, width), bf16),
            pltpu.VMEM((width, main), bf16),
            pltpu.VMEM((width, 2 * (cols - main)), bf16),
            pltpu.VMEM((cols, rows), bf16),
            pltpu.VMEM((cols + VALUE_PADDING, half), bf16),
            pltpu.VMEM((1, cols), f32),
            pltpu.VMEM((1, cols), f32),
            pltpu.SMEM((3,), jnp.int32),
        ),
        in_specs=[HBM] * 9,
        out_specs=(VMEM,) * 7 + (SMEM,),
        scratch_shapes=[
            pltpu.SMEM((2,), jnp.int32),
            pltpu.SMEM((2,), jnp.int32),
            pltpu.VMEM((rows, width), bf16),
            pltpu.VMEM((width, cols), bf16),
            pltpu.VMEM(level_table.shape, bf16),
            pltpu.VMEM((2, width), f32),
            pltpu.VMEM((2, width), f32),
            pltpu.SemaphoreType.DMA((5,)),
            pltpu.SemaphoreType.DMA((4,)),
            pltpu.SemaphoreType.DMA((5,)),
        ],
        compiler_params=pltpu.CompilerParams(vmem_limit_bytes=22 * MIB),
        cost_estimate=pl.CostEstimate(
            flops=2 * rows * width * cols, bytes_accessed=26_000_000, transcendentals=0
        ),
        name="project_value",
    )(*operands)


def query_key_kernel(shaped, key_weights, mixed_weights, w_query, query, key, sums_out, weights, sem):
    cols = query.shape[1]
    main = key_weights.shape[1]
    rest = cols - main
    fetch = pltpu.make_async_copy(w_query.at[:, pl.ds(rest, main)], weights, sem.at[0])
    fetch.start()

    def dot(w):
        return jnp.dot(shaped[...], w[...], preferred_element_type=jnp.float32)

    key[:, :main] = dot(key_weights)
    middle = dot(mixed_weights)
    key[:, main:] = middle[:, :rest]
    query[:, :rest] = middle[:, rest:]
    fetch.wait()
    query[:, rest:] = dot(weights)
    for at, ref in ((0, key), (4, query)):
        x = ref[...]
        sums_out[at : at + 4, :] = as_rows(jnp.sum(x * x, axis=1, keepdims=True))


def project_query_key(shaped, key_weights, mixed_weights, w_query):
    rows, width = shaped.shape
    cols = w_query.shape[1]
    f32 = jnp.float32
    return pl.pallas_call(
        query_key_kernel,
        out_shape=(
            pltpu.VMEM((rows, cols), f32),
            pltpu.VMEM((rows, cols), f32),
            pltpu.VMEM((8, 128), f32),
        ),
        in_specs=[VMEM] * 3 + [HBM],
        out_specs=(VMEM,) * 3,
        scratch_shapes=[pltpu.VMEM(key_weights.shape, jnp.bfloat16), pltpu.SemaphoreType.DMA((1,))],
        compiler_params=pltpu.CompilerParams(vmem_limit_bytes=16 * MIB),
        cost_estimate=pl.CostEstimate(
            flops=4 * rows * width * cols, bytes_accessed=18_000_000, transcendentals=0
        ),
        name="project_query_key",
    )(shaped, key_weights, mixed_weights, pltpu.with_memory_space_constraint(w_query, pltpu.HBM))


def norm_factor(sums, at, total_cols):
    first, second, third, fourth = (x[at : at + 4, :] for x in sums)
    return as_columns(lax.rsqrt((first + second + (third + fourth)) / total_cols + EPSILON))


def key_kernel(total_cols, key, gain, s0, s1, s2, s3, all_out, early, late, passed):
    factor = norm_factor((s0, s1, s2, s3), 0, total_cols)
    half = early.shape[0]
    for c in range(0, key.shape[1], 128):
        normed = (key[:, c : c + 128] * factor * gain[0:1, c : c + 128]).astype(jnp.bfloat16)
        all_out[:, c : c + 128] = normed
        late[:half, c : c + 128] = normed[:half]
        late[half:, c : c + 128] = normed[: 2 * PADDING]
        early[:, c : c + 128] = normed[half:]
        passed[:half, c : c + 128] = normed[half:]
        passed[half:, c : c + 128] = normed[-PADDING:]


def normalise_key(key, gain, sums, total_cols):
    rows, cols = key.shape
    bf16 = jnp.bfloat16
    return pl.pallas_call(
        functools.partial(key_kernel, total_cols),
        out_shape=(
            jax.ShapeDtypeStruct((rows, cols), bf16),
            jax.ShapeDtypeStruct((rows // 2, cols), bf16),
            jax.ShapeDtypeStruct((rows // 2 + 2 * PADDING, cols), bf16),
            jax.ShapeDtypeStruct((rows // 2 + PADDING, cols), bf16),
        ),
        in_specs=[VMEM] * 6,
        out_specs=(VMEM,) * 4,
        compiler_params=pltpu.CompilerParams(vmem_limit_bytes=12 * MIB),
        cost_estimate=pl.CostEstimate(flops=2 * rows * cols, bytes_accessed=100_000, transcendentals=0),
        name="normalise_key",
    )(key, gain, *sums)


def attend_block(first, q, k, vt, acc, peak, mass):
    heads = q.shape[1] // HD
    cols = [slice(h * HD, (h + 1) * HD) for h in range(heads)]
    scores = [
        lax.dot_general(k[:, c], q[:, c], (((1,), (1,)), ((), ())), preferred_element_type=jnp.float32)
        for c in cols
    ]
    tops = [jnp.max(s, axis=0, keepdims=True) for s in scores]
    if not first:
        olds = [peak[h : h + 1, :] for h in range(heads)]
        tops = [jnp.maximum(t, o) for t, o in zip(tops, olds)]
        fades = [jnp.exp2((o - t) * EXP2_SCALE) for t, o in zip(tops, olds)]
    expos = [jnp.exp2((s - t) * EXP2_SCALE) for s, t in zip(scores, tops)]
    for h in range(heads):
        total = jnp.sum(expos[h], axis=0, keepdims=True)
        peak[h : h + 1, :] = tops[h]
        mass[h : h + 1, :] = total if first else mass[h : h + 1, :] * fades[h] + total
    for h, c in enumerate(cols):
        part = jnp.dot(vt[c, :], expos[h].astype(jnp.bfloat16), preferred_element_type=jnp.float32)
        acc[c, :] = part if first else acc[c, :] * fades[h] + part


def local_kernel(
    total_cols, info, query, gain, s0, s1, s2, s3, key, value, query_out, acc, peak, mass,
):
    factor = norm_factor((s0, s1, s2, s3), 4, total_cols)
    for c in range(0, query.shape[1], 128):
        query_out[:, c : c + 128] = (
            query[:, c : c + 128] * factor * gain[0:1, c : c + 128]
        ).astype(jnp.bfloat16)
    frame = query.shape[0] // 2
    at = [pl.ds(0, frame), pl.ds(frame, frame)]
    for f in range(2):
        attend_block(
            True, query_out.at[at[f]], key.at[at[f]], value.at[:, at[f]],
            acc.at[f], peak.at[f], mass.at[f],
        )

    @pl.when(info[1] >= 1)
    def _():
        attend_block(
            False, query_out.at[at[1]], key.at[at[0]], value.at[:, at[0]],
            acc.at[1], peak.at[1], mass.at[1],
        )


def local_attention(info, query, gain, sums, key, value, total_cols):
    rows, cols = query.shape
    f32 = jnp.float32
    return pl.pallas_call(
        functools.partial(local_kernel, total_cols),
        out_shape=(
            pltpu.VMEM((rows, cols), jnp.bfloat16),
            pltpu.VMEM((2, cols, rows // 2), f32),
            pltpu.VMEM((2, 8, rows // 2), f32),
            pltpu.VMEM((2, 8, rows // 2), f32),
        ),
        in_specs=[SMEM] + [VMEM] * 8,
        out_specs=(VMEM,) * 4,
        compiler_params=pltpu.CompilerParams(vmem_limit_bytes=12 * MIB),
        cost_estimate=pl.CostEstimate(flops=3_000_000, bytes_accessed=100_000, transcendentals=0),
        name="local_attention",
    )(info, query, gain, *sums, key, value)


def near_kernel(g, info, query, acc_in, peak_in, mass_in, keys, values, acc, peak, mass):
    frame = query.shape[0] // 2
    at = [pl.ds(0, frame), pl.ds(frame, frame)]
    for f in range(2):

        @pl.when(info[f] >= f + 2 - g)
        def _():
            attend_block(
                False, query.at[at[f]], keys.at[at[0]], values.at[:, at[g]],
                acc.at[f], peak.at[f], mass.at[f],
            )


def near_attention(g, info, query, acc, peak, mass, keys, values):
    rows, cols = query.shape
    f32 = jnp.float32
    return pl.pallas_call(
        functools.partial(near_kernel, g),
        out_shape=(
            pltpu.VMEM((2, cols, rows // 2), f32),
            pltpu.VMEM((2, 8, rows // 2), f32),
            pltpu.VMEM((2, 8, rows // 2), f32),
        ),
        in_specs=[SMEM] + [VMEM] * 6,
        out_specs=(VMEM,) * 3,
        input_output_aliases={2: 0, 3: 1, 4: 2},
        compiler_params=pltpu.CompilerParams(vmem_limit_bytes=12 * MIB),
        cost_estimate=pl.CostEstimate(flops=1_000_000, bytes_accessed=100_000, transcendentals=0),
        name="near_attention",
    )(info, query, acc, peak, mass, keys, values)


def far_kernel(
    info, query, acc_in, peak_in, mass_in, far_keys, far_values, relayed_keys, relayed_values,
    out, acc, peak, mass,
):
    cols = query.shape[1]
    frame = query.shape[0] // 2
    at = [pl.ds(0, frame), pl.ds(frame, frame)]
    acc[...] = acc_in[0]
    peak[...] = peak_in[0]
    mass[...] = mass_in[0]
    for core, k, v in (
        (0, far_keys.at[at[0]], far_values),
        (1, relayed_keys, relayed_values.at[:, at[1]]),
    ):

        @pl.when(jnp.logical_and(info[2] == core, info[0] >= 3))
        def _():
            attend_block(False, query.at[at[0]], k, v, acc, peak, mass)

    for f in range(2):
        for h in range(cols // HD):
            c = slice(h * HD, (h + 1) * HD)
            if f == 0:
                result = acc[c, :] / mass[h : h + 1, :]
            else:
                result = acc_in[f, c, :] / mass_in[f, h : h + 1, :]
            out[at[f], c] = jnp.transpose(result).astype(out.dtype)


def far_attention(info, query, acc, peak, mass, halo):
    rows, cols = query.shape
    f32 = jnp.float32
    stats = pltpu.VMEM((8, rows // 2), f32)
    return pl.pallas_call(
        far_kernel,
        out_shape=jax.ShapeDtypeStruct((rows, cols), jnp.bfloat16),
        in_specs=[SMEM] + [VMEM] * 8,
        out_specs=VMEM,
        scratch_shapes=[pltpu.VMEM((cols, rows // 2), f32), stats, stats],
        compiler_params=pltpu.CompilerParams(vmem_limit_bytes=12 * MIB),
        cost_estimate=pl.CostEstimate(flops=1_000_000, bytes_accessed=100_000, transcendentals=0),
        name="far_attention",
    )(info, query, acc, peak, mass, *halo)


def on_device(
    latents, noise_level, lookback, level_table, w_query, w_key, w_value, gain_query, gain_key
):
    devices = lax.axis_size("queue")
    members = lax.axis_size("tp")
    total_cols = w_query.shape[1] * members
    along = [(i, (i + 1) % devices) for i in range(devices)]
    swap = [(i, i ^ 1) for i in range(devices)]

    def facing(i, t):
        if i in (0, devices - 1):
            return i * members + (t ^ 1)
        return (i + 1 if i % 2 else i - 1) * members + t

    across = [(i * members + t, facing(i, t)) for i in range(devices) for t in range(members)]

    def move(x, pairs):
        return lax.ppermute(x, "queue", pairs)

    def move_across(x):
        return lax.ppermute(x, ("queue", "tp"), across)

    shaped, key_weights, mixed_weights, value, value_early, gain_query, gain_key, info = project_value(
        noise_level, lookback, latents, level_table, w_query, w_key, w_value, gain_query, gain_key
    )
    info = pltpu.with_memory_space_constraint(info, pltpu.SMEM)
    near_value = move(value, along)
    pair_value = move(value_early, swap)
    query, key, sums = project_query_key(shaped, key_weights, mixed_weights, w_query)
    pair_value, sums = lax.optimization_barrier((pair_value, sums))
    sums = [sums] + [
        lax.ppermute(sums, "tp", pairs)
        for pairs in (
            [(0, 1), (1, 0), (2, 3), (3, 2)],
            [(0, 3), (3, 0), (1, 2), (2, 1)],
            [(0, 2), (2, 0), (1, 3), (3, 1)],
        )
    ]
    far_value = move(pair_value, along)
    key_normed, key_early, key_late, key_passed = normalise_key(key, gain_key, sums, total_cols)
    key_normed, near_value = lax.optimization_barrier((key_normed, near_value))
    relayed_value = move(near_value, swap)
    near_key = move(key_early, along)
    mid_key = move(key_late, along)
    pair_key = move(key_passed, swap)
    far_key = move_across(pair_key)
    key_normed, pair_key = lax.optimization_barrier((key_normed, pair_key))
    query_normed, acc, peak, mass = local_attention(
        info, query, gain_query, sums, key_normed, value, total_cols
    )
    near_key, acc, far_value = lax.optimization_barrier((near_key, acc, far_value))
    relayed_key = move(near_key, swap)
    acc, peak, mass = near_attention(1, info, query_normed, acc, peak, mass, near_key, near_value)
    acc, peak, mass = near_attention(0, info, query_normed, acc, peak, mass, mid_key, near_value)
    return far_attention(
        info, query_normed, acc, peak, mass, (far_key, far_value, relayed_key, relayed_value)
    )


def solution(mesh):
    in_specs = (
        P("queue", None),
        P("queue"),
        P("queue"),
        P(),
        P(None, "tp"),
        P(None, "tp"),
        P(None, "tp"),
        P("tp"),
        P("tp"),
    )
    return jax.shard_map(
        on_device, mesh=mesh, in_specs=in_specs, out_specs=P("queue", "tp"), check_vma=False
    )
```

```python
import functools

import jax
import jax.numpy as jnp
from jax import lax
from jax.experimental import pallas as pl
from jax.experimental.pallas import tpu as pltpu
from jax.sharding import PartitionSpec as P

HD = 128
WIN = 4
EPSILON = 1e-06
MIB = 2**20
VALUE_PADDING = 80
PADDING = 16
EXP2_SCALE = HD ** (-0.5) * 1.4426950408889634

HBM = pl.BlockSpec(memory_space=pltpu.HBM)
VMEM = pl.BlockSpec(memory_space=pltpu.VMEM)
SMEM = pl.BlockSpec(memory_space=pltpu.SMEM)


def as_rows(column):
    wide = jnp.broadcast_to(column, (column.shape[0], 128))
    parts = [
        jnp.transpose(wide[i : i + 128])[0:1] for i in range(0, column.shape[0], 128)
    ]
    return jnp.concatenate(parts, 0)


def as_columns(rows):
    parts = [
        jnp.transpose(jnp.broadcast_to(rows[i : i + 1], (128, 128)))
        for i in range(rows.shape[0])
    ]
    return jnp.concatenate(parts, 0)


def value_kernel(
    noise_level, lookback, latents, level_table, w_query, w_key, w_value, gain_query, gain_key,
    shaped, key_weights, mixed_weights, value_both, value_early, gains_query, gains_key, info,
    levels, reaches, lat, weights, table, shift, scale, small_sem, lat_sem, w_sem,
):
    width = latents.shape[1]
    frame = latents.shape[0] // 2
    half = frame // 2
    cols = w_value.shape[1]
    main = key_weights.shape[1]
    rest = cols - main
    small = [
        pltpu.make_async_copy(src, dst, small_sem.at[i])
        for i, (src, dst) in enumerate(
            (
                (noise_level, levels),
                (level_table, table),
                (lookback, reaches),
                (gain_query, gains_query.at[0]),
                (gain_key, gains_key.at[0]),
            )
        )
    ]
    lat_copies = [
        pltpu.make_async_copy(
            latents.at[pl.ds(c * half, half)], lat.at[pl.ds(c * half, half)], lat_sem.at[c]
        )
        for c in range(4)
    ]
    for copy in lat_copies[:1] + small[:2] + lat_copies[1:] + small[2:]:
        copy.start()
    fetches = [
        pltpu.make_async_copy(src, dst, w_sem.at[i])
        for i, (src, dst) in enumerate(
            (
                (w_value.at[:, pl.ds(0, 256)], weights.at[:, pl.ds(0, 256)]),
                (w_value.at[:, pl.ds(256, 384)], weights.at[:, pl.ds(256, 384)]),
                (w_key.at[:, pl.ds(0, main)], key_weights),
                (w_key.at[:, pl.ds(main, rest)], mixed_weights.at[:, pl.ds(0, rest)]),
                (w_query.at[:, pl.ds(0, rest)], mixed_weights.at[:, pl.ds(rest, rest)]),
            )
        )
    ]

    for copy in small[:2]:
        copy.wait()
    pick = lax.broadcasted_iota(jnp.int32, (8, 1), 0)
    wanted = jnp.where(pick == 0, levels[0], levels[1])
    chosen = lax.broadcasted_iota(jnp.int32, (8, table.shape[0]), 1) == wanted
    rows = jnp.dot(
        chosen.astype(jnp.float32).astype(jnp.bfloat16), table[...], preferred_element_type=jnp.float32
    )
    shift[...] = rows[0:2, :width]
    scale[...] = 1.0 + rows[0:2, width:]

    def shape_rows(f, start, count):
        rows = slice(start, start + count)
        x = lat[rows, :].astype(jnp.float32)
        center = jnp.mean(x, axis=1, keepdims=True)
        x = x - center
        spread = jnp.mean(x * x, axis=1, keepdims=True)
        x = x * lax.rsqrt(spread + EPSILON)
        shaped[rows, :] = (x * scale[f : f + 1, :] + shift[f : f + 1, :]).astype(jnp.bfloat16)

    def value_rows(f):
        rows = slice(f * frame, (f + 1) * frame)
        result = jnp.dot(shaped[rows, :], weights[...], preferred_element_type=jnp.float32)
        turned = jnp.transpose(result).astype(jnp.bfloat16)
        value_both[:, rows] = turned
        if f == 1:
            value_early[:cols, :] = turned
            value_early[cols:, :] = turned[:VALUE_PADDING]

    group = 64
    for c in range(2):
        lat_copies[c].wait()
        fetches[c].start()
        for j in range(c * half, (c + 1) * half, group):
            shape_rows(0, j, group)
    for c in range(2, 4):
        lat_copies[c].wait()
        fetches[c].start()
    fetches[4].start()
    fetches[0].wait()
    fetches[1].wait()
    for j in range(frame, 2 * frame, group):
        shape_rows(1, j, group)
    value_rows(0)
    value_rows(1)
    for copy in small[2:]:
        copy.wait()
    info[0] = reaches[0]
    info[1] = reaches[1]
    info[2] = lax.rem(lax.axis_index("queue"), 2)
    for copy in fetches[2:]:
        copy.wait()


def project_value(noise_level, lookback, latents, level_table, w_query, w_key, w_value, gain_query, gain_key):
    rows, width = latents.shape
    cols = w_query.shape[1]
    half = rows // 2
    main = cols // 256 * 256
    f32, bf16 = jnp.float32, jnp.bfloat16
    operands = (
        noise_level, lookback, latents, level_table, w_query, w_key, w_value, gain_query, gain_key
    )
    operands = [pltpu.with_memory_space_constraint(x, pltpu.HBM) for x in operands]
    return pl.pallas_call(
        value_kernel,
        out_shape=(
            pltpu.VMEM((rows, width), bf16),
            pltpu.VMEM((width, main), bf16),
            pltpu.VMEM((width, 2 * (cols - main)), bf16),
            pltpu.VMEM((cols, rows), bf16),
            pltpu.VMEM((cols + VALUE_PADDING, half), bf16),
            pltpu.VMEM((1, cols), f32),
            pltpu.VMEM((1, cols), f32),
            pltpu.SMEM((3,), jnp.int32),
        ),
        in_specs=[HBM] * 9,
        out_specs=(VMEM,) * 7 + (SMEM,),
        scratch_shapes=[
            pltpu.SMEM((2,), jnp.int32),
            pltpu.SMEM((2,), jnp.int32),
            pltpu.VMEM((rows, width), bf16),
            pltpu.VMEM((width, cols), bf16),
            pltpu.VMEM(level_table.shape, bf16),
            pltpu.VMEM((2, width), f32),
            pltpu.VMEM((2, width), f32),
            pltpu.SemaphoreType.DMA((5,)),
            pltpu.SemaphoreType.DMA((4,)),
            pltpu.SemaphoreType.DMA((5,)),
        ],
        compiler_params=pltpu.CompilerParams(vmem_limit_bytes=22 * MIB),
        cost_estimate=pl.CostEstimate(
            flops=2 * rows * width * cols, bytes_accessed=26_000_000, transcendentals=0
        ),
        name="project_value",
    )(*operands)


def query_key_kernel(shaped, key_weights, mixed_weights, w_query, query, key, sums_out, weights, sem):
    cols = query.shape[1]
    main = key_weights.shape[1]
    rest = cols - main
    fetch = pltpu.make_async_copy(w_query.at[:, pl.ds(rest, main)], weights, sem.at[0])
    fetch.start()

    def dot(w):
        return jnp.dot(shaped[...], w[...], preferred_element_type=jnp.float32)

    key[:, :main] = dot(key_weights)
    middle = dot(mixed_weights)
    key[:, main:] = middle[:, :rest]
    query[:, :rest] = middle[:, rest:]
    fetch.wait()
    query[:, rest:] = dot(weights)
    for at, ref in ((0, key), (4, query)):
        x = ref[...]
        sums_out[at : at + 4, :] = as_rows(jnp.sum(x * x, axis=1, keepdims=True))


def project_query_key(shaped, key_weights, mixed_weights, w_query):
    rows, width = shaped.shape
    cols = w_query.shape[1]
    f32 = jnp.float32
    return pl.pallas_call(
        query_key_kernel,
        out_shape=(
            pltpu.VMEM((rows, cols), f32),
            pltpu.VMEM((rows, cols), f32),
            pltpu.VMEM((8, 128), f32),
        ),
        in_specs=[VMEM] * 3 + [HBM],
        out_specs=(VMEM,) * 3,
        scratch_shapes=[pltpu.VMEM(key_weights.shape, jnp.bfloat16), pltpu.SemaphoreType.DMA((1,))],
        compiler_params=pltpu.CompilerParams(vmem_limit_bytes=16 * MIB),
        cost_estimate=pl.CostEstimate(
            flops=4 * rows * width * cols, bytes_accessed=18_000_000, transcendentals=0
        ),
        name="project_query_key",
    )(shaped, key_weights, mixed_weights, pltpu.with_memory_space_constraint(w_query, pltpu.HBM))


def norm_factor(sums, at, total_cols):
    first, second, third, fourth = (x[at : at + 4, :] for x in sums)
    return as_columns(lax.rsqrt((first + second + (third + fourth)) / total_cols + EPSILON))


def later_kernel(value, out):
    cols, frame = out.shape
    out[...] = value[:cols, frame:]


def later_frame(value, cols):
    return pl.pallas_call(
        later_kernel,
        out_shape=pltpu.VMEM((cols, value.shape[1] // 2), jnp.bfloat16),
        in_specs=[VMEM],
        out_specs=VMEM,
        compiler_params=pltpu.CompilerParams(vmem_limit_bytes=8 * MIB),
        cost_estimate=pl.CostEstimate(flops=1000, bytes_accessed=1000, transcendentals=0),
        name="later_frame",
    )(value)


def key_kernel(total_cols, key, gain, s0, s1, s2, s3, all_out, early, late, passed):
    factor = norm_factor((s0, s1, s2, s3), 0, total_cols)
    half = early.shape[0]
    for c in range(0, key.shape[1], 128):
        normed = (key[:, c : c + 128] * factor * gain[0:1, c : c + 128]).astype(jnp.bfloat16)
        all_out[:, c : c + 128] = normed
        late[:half, c : c + 128] = normed[:half]
        late[half:, c : c + 128] = normed[: 2 * PADDING]
        early[:, c : c + 128] = normed[half:]
        passed[:half, c : c + 128] = normed[half:]
        passed[half:, c : c + 128] = normed[-PADDING:]


def normalise_key(key, gain, sums, total_cols):
    rows, cols = key.shape
    bf16 = jnp.bfloat16
    return pl.pallas_call(
        functools.partial(key_kernel, total_cols),
        out_shape=(
            jax.ShapeDtypeStruct((rows, cols), bf16),
            jax.ShapeDtypeStruct((rows // 2, cols), bf16),
            jax.ShapeDtypeStruct((rows // 2 + 2 * PADDING, cols), bf16),
            jax.ShapeDtypeStruct((rows // 2 + PADDING, cols), bf16),
        ),
        in_specs=[VMEM] * 6,
        out_specs=(VMEM,) * 4,
        compiler_params=pltpu.CompilerParams(vmem_limit_bytes=12 * MIB),
        cost_estimate=pl.CostEstimate(flops=2 * rows * cols, bytes_accessed=100_000, transcendentals=0),
        name="normalise_key",
    )(key, gain, *sums)


def attend_block(first, q, k, vt, acc, peak, mass):
    heads = q.shape[1] // HD
    cols = [slice(h * HD, (h + 1) * HD) for h in range(heads)]
    scores = [
        lax.dot_general(k[:, c], q[:, c], (((1,), (1,)), ((), ())), preferred_element_type=jnp.float32)
        for c in cols
    ]
    tops = [jnp.max(s, axis=0, keepdims=True) for s in scores]
    if not first:
        olds = [peak[h : h + 1, :] for h in range(heads)]
        tops = [jnp.maximum(t, o) for t, o in zip(tops, olds)]
        fades = [jnp.exp2((o - t) * EXP2_SCALE) for t, o in zip(tops, olds)]
    expos = [jnp.exp2((s - t) * EXP2_SCALE) for s, t in zip(scores, tops)]
    for h in range(heads):
        total = jnp.sum(expos[h], axis=0, keepdims=True)
        peak[h : h + 1, :] = tops[h]
        mass[h : h + 1, :] = total if first else mass[h : h + 1, :] * fades[h] + total
    for h, c in enumerate(cols):
        part = jnp.dot(vt[c, :], expos[h].astype(jnp.bfloat16), preferred_element_type=jnp.float32)
        acc[c, :] = part if first else acc[c, :] * fades[h] + part


def local_kernel(
    total_cols, info, query, gain, s0, s1, s2, s3, key, value, query_out, acc, peak, mass,
):
    factor = norm_factor((s0, s1, s2, s3), 4, total_cols)
    for c in range(0, query.shape[1], 128):
        query_out[:, c : c + 128] = (
            query[:, c : c + 128] * factor * gain[0:1, c : c + 128]
        ).astype(jnp.bfloat16)
    frame = query.shape[0] // 2
    at = [pl.ds(0, frame), pl.ds(frame, frame)]
    for f in range(2):
        attend_block(
            True, query_out.at[at[f]], key.at[at[f]], value.at[:, at[f]],
            acc.at[f], peak.at[f], mass.at[f],
        )

    @pl.when(info[1] >= 1)
    def _():
        attend_block(
            False, query_out.at[at[1]], key.at[at[0]], value.at[:, at[0]],
            acc.at[1], peak.at[1], mass.at[1],
        )


def local_attention(info, query, gain, sums, key, value, total_cols):
    rows, cols = query.shape
    f32 = jnp.float32
    return pl.pallas_call(
        functools.partial(local_kernel, total_cols),
        out_shape=(
            pltpu.VMEM((rows, cols), jnp.bfloat16),
            pltpu.VMEM((2, cols, rows // 2), f32),
            pltpu.VMEM((2, 8, rows // 2), f32),
            pltpu.VMEM((2, 8, rows // 2), f32),
        ),
        in_specs=[SMEM] + [VMEM] * 8,
        out_specs=(VMEM,) * 4,
        compiler_params=pltpu.CompilerParams(vmem_limit_bytes=12 * MIB),
        cost_estimate=pl.CostEstimate(flops=3_000_000, bytes_accessed=100_000, transcendentals=0),
        name="local_attention",
    )(info, query, gain, *sums, key, value)


def near_kernel(g, info, query, acc_in, peak_in, mass_in, keys, values, acc, peak, mass):
    frame = query.shape[0] // 2
    at = [pl.ds(0, frame), pl.ds(frame, frame)]
    for f in range(2):

        @pl.when(info[f] >= f + 2 - g)
        def _():
            attend_block(
                False, query.at[at[f]], keys.at[at[0]], values.at[:, at[g]],
                acc.at[f], peak.at[f], mass.at[f],
            )


def near_attention(g, info, query, acc, peak, mass, keys, values):
    rows, cols = query.shape
    f32 = jnp.float32
    return pl.pallas_call(
        functools.partial(near_kernel, g),
        out_shape=(
            pltpu.VMEM((2, cols, rows // 2), f32),
            pltpu.VMEM((2, 8, rows // 2), f32),
            pltpu.VMEM((2, 8, rows // 2), f32),
        ),
        in_specs=[SMEM] + [VMEM] * 6,
        out_specs=(VMEM,) * 3,
        input_output_aliases={2: 0, 3: 1, 4: 2},
        compiler_params=pltpu.CompilerParams(vmem_limit_bytes=12 * MIB),
        cost_estimate=pl.CostEstimate(flops=1_000_000, bytes_accessed=100_000, transcendentals=0),
        name="near_attention",
    )(info, query, acc, peak, mass, keys, values)


def far_kernel(
    info, query, acc_in, peak_in, mass_in, far_keys, far_values, relayed_keys, relayed_values,
    out, acc, peak, mass,
):
    cols = query.shape[1]
    frame = query.shape[0] // 2
    at = [pl.ds(0, frame), pl.ds(frame, frame)]
    acc[...] = acc_in[0]
    peak[...] = peak_in[0]
    mass[...] = mass_in[0]
    for core, k, v in (
        (0, far_keys.at[at[0]], far_values),
        (1, relayed_keys, relayed_values),
    ):

        @pl.when(jnp.logical_and(info[2] == core, info[0] >= 3))
        def _():
            attend_block(False, query.at[at[0]], k, v, acc, peak, mass)

    for f in range(2):
        for h in range(cols // HD):
            c = slice(h * HD, (h + 1) * HD)
            if f == 0:
                result = acc[c, :] / mass[h : h + 1, :]
            else:
                result = acc_in[f, c, :] / mass_in[f, h : h + 1, :]
            out[at[f], c] = jnp.transpose(result).astype(out.dtype)


def far_attention(info, query, acc, peak, mass, halo):
    rows, cols = query.shape
    f32 = jnp.float32
    stats = pltpu.VMEM((8, rows // 2), f32)
    return pl.pallas_call(
        far_kernel,
        out_shape=jax.ShapeDtypeStruct((rows, cols), jnp.bfloat16),
        in_specs=[SMEM] + [VMEM] * 8,
        out_specs=VMEM,
        scratch_shapes=[pltpu.VMEM((cols, rows // 2), f32), stats, stats],
        compiler_params=pltpu.CompilerParams(vmem_limit_bytes=12 * MIB),
        cost_estimate=pl.CostEstimate(flops=1_000_000, bytes_accessed=100_000, transcendentals=0),
        name="far_attention",
    )(info, query, acc, peak, mass, *halo)


def on_device(
    latents, noise_level, lookback, level_table, w_query, w_key, w_value, gain_query, gain_key
):
    devices = lax.axis_size("queue")
    members = lax.axis_size("tp")
    total_cols = w_query.shape[1] * members
    along = [(i, (i + 1) % devices) for i in range(devices)]
    swap = [(i, i ^ 1) for i in range(devices)]

    def facing(i, t):
        if i in (0, devices - 1):
            return i * members + (t ^ 1)
        return (i + 1 if i % 2 else i - 1) * members + t

    across = [(i * members + t, facing(i, t)) for i in range(devices) for t in range(members)]

    def move(x, pairs):
        return lax.ppermute(x, "queue", pairs)

    def move_across(x):
        return lax.ppermute(x, ("queue", "tp"), across)

    shaped, key_weights, mixed_weights, value, value_early, gain_query, gain_key, info = project_value(
        noise_level, lookback, latents, level_table, w_query, w_key, w_value, gain_query, gain_key
    )
    info = pltpu.with_memory_space_constraint(info, pltpu.SMEM)
    near_value = move(value, along)
    pair_value = move(value_early, swap)
    query, key, sums = project_query_key(shaped, key_weights, mixed_weights, w_query)
    pair_value, sums = lax.optimization_barrier((pair_value, sums))
    sums = [sums] + [
        lax.ppermute(sums, "tp", pairs)
        for pairs in (
            [(0, 1), (1, 0), (2, 3), (3, 2)],
            [(0, 3), (3, 0), (1, 2), (2, 1)],
            [(0, 2), (2, 0), (1, 3), (3, 1)],
        )
    ]
    far_value = move(pair_value, along)
    key_normed, key_early, key_late, key_passed = normalise_key(key, gain_key, sums, total_cols)
    key_normed, near_value = lax.optimization_barrier((key_normed, near_value))
    relayed_value = move(later_frame(near_value, key.shape[1]), swap)
    near_key = move(key_early, along)
    mid_key = move(key_late, along)
    pair_key = move(key_passed, swap)
    far_key = move_across(pair_key)
    key_normed, pair_key = lax.optimization_barrier((key_normed, pair_key))
    query_normed, acc, peak, mass = local_attention(
        info, query, gain_query, sums, key_normed, value, total_cols
    )
    near_key, acc, far_value = lax.optimization_barrier((near_key, acc, far_value))
    relayed_key = move(near_key, swap)
    acc, peak, mass = near_attention(1, info, query_normed, acc, peak, mass, near_key, near_value)
    acc, peak, mass = near_attention(0, info, query_normed, acc, peak, mass, mid_key, near_value)
    return far_attention(
        info, query_normed, acc, peak, mass, (far_key, far_value, relayed_key, relayed_value)
    )


def solution(mesh):
    in_specs = (
        P("queue", None),
        P("queue"),
        P("queue"),
        P(),
        P(None, "tp"),
        P(None, "tp"),
        P(None, "tp"),
        P("tp"),
        P("tp"),
    )
    return jax.shard_map(
        on_device, mesh=mesh, in_specs=in_specs, out_specs=P("queue", "tp"), check_vma=False
    )
```

```python
import functools

import jax
import jax.numpy as jnp
from jax import lax
from jax.experimental import pallas as pl
from jax.experimental.pallas import tpu as pltpu
from jax.sharding import PartitionSpec as P

HD = 128
WIN = 4
EPSILON = 1e-06
MIB = 2**20
VALUE_PADDING = 80
PADDING = 16
EXP2_SCALE = HD ** (-0.5) * 1.4426950408889634

HBM = pl.BlockSpec(memory_space=pltpu.HBM)
VMEM = pl.BlockSpec(memory_space=pltpu.VMEM)
SMEM = pl.BlockSpec(memory_space=pltpu.SMEM)


def as_rows(column):
    wide = jnp.broadcast_to(column, (column.shape[0], 128))
    parts = [
        jnp.transpose(wide[i : i + 128])[0:1] for i in range(0, column.shape[0], 128)
    ]
    return jnp.concatenate(parts, 0)


def as_columns(rows):
    parts = [
        jnp.transpose(jnp.broadcast_to(rows[i : i + 1], (128, 128)))
        for i in range(rows.shape[0])
    ]
    return jnp.concatenate(parts, 0)


def value_kernel(
    noise_level, lookback, latents, level_table, w_query, w_key, w_value, gain_query, gain_key,
    shaped, key_weights, mixed_weights, value_both, value_early, gains_query, gains_key, info,
    levels, reaches, lat, weights, table, shift, scale, small_sem, lat_sem, w_sem,
):
    width = latents.shape[1]
    frame = latents.shape[0] // 2
    half = frame // 2
    cols = w_value.shape[1]
    main = key_weights.shape[1]
    rest = cols - main
    small = [
        pltpu.make_async_copy(src, dst, small_sem.at[i])
        for i, (src, dst) in enumerate(
            (
                (noise_level, levels),
                (level_table, table),
                (lookback, reaches),
                (gain_query, gains_query.at[0]),
                (gain_key, gains_key.at[0]),
            )
        )
    ]
    lat_copies = [
        pltpu.make_async_copy(
            latents.at[pl.ds(c * half, half)], lat.at[pl.ds(c * half, half)], lat_sem.at[c]
        )
        for c in range(4)
    ]
    for copy in lat_copies[:1] + small[:2] + lat_copies[1:] + small[2:]:
        copy.start()
    fetches = [
        pltpu.make_async_copy(src, dst, w_sem.at[i])
        for i, (src, dst) in enumerate(
            (
                (w_value.at[:, pl.ds(0, 256)], weights.at[:, pl.ds(0, 256)]),
                (w_value.at[:, pl.ds(256, 384)], weights.at[:, pl.ds(256, 384)]),
                (w_key.at[:, pl.ds(0, main)], key_weights),
                (w_key.at[:, pl.ds(main, rest)], mixed_weights.at[:, pl.ds(0, rest)]),
                (w_query.at[:, pl.ds(0, rest)], mixed_weights.at[:, pl.ds(rest, rest)]),
            )
        )
    ]

    for copy in small[:2]:
        copy.wait()
    pick = lax.broadcasted_iota(jnp.int32, (8, 1), 0)
    wanted = jnp.where(pick == 0, levels[0], levels[1])
    chosen = lax.broadcasted_iota(jnp.int32, (8, table.shape[0]), 1) == wanted
    rows = jnp.dot(
        chosen.astype(jnp.float32).astype(jnp.bfloat16), table[...], preferred_element_type=jnp.float32
    )
    shift[...] = rows[0:2, :width]
    scale[...] = 1.0 + rows[0:2, width:]

    def shape_rows(f, start, count):
        rows = slice(start, start + count)
        x = lat[rows, :].astype(jnp.float32)
        center = jnp.mean(x, axis=1, keepdims=True)
        x = x - center
        spread = jnp.mean(x * x, axis=1, keepdims=True)
        x = x * lax.rsqrt(spread + EPSILON)
        shaped[rows, :] = (x * scale[f : f + 1, :] + shift[f : f + 1, :]).astype(jnp.bfloat16)

    def value_rows(f):
        rows = slice(f * frame, (f + 1) * frame)
        result = jnp.dot(shaped[rows, :], weights[...], preferred_element_type=jnp.float32)
        turned = jnp.transpose(result).astype(jnp.bfloat16)
        value_both[:, rows] = turned
        if f == 1:
            value_early[:cols, :] = turned
            value_early[cols:, :] = turned[:VALUE_PADDING]

    group = 64
    for c in range(2):
        lat_copies[c].wait()
        fetches[c].start()
        for j in range(c * half, (c + 1) * half, group):
            shape_rows(0, j, group)
    for c in range(2, 4):
        lat_copies[c].wait()
        fetches[c].start()
    fetches[4].start()
    fetches[0].wait()
    fetches[1].wait()
    for j in range(frame, 2 * frame, group):
        shape_rows(1, j, group)
    value_rows(0)
    value_rows(1)
    for copy in small[2:]:
        copy.wait()
    info[0] = reaches[0]
    info[1] = reaches[1]
    info[2] = lax.rem(lax.axis_index("queue"), 2)
    for copy in fetches[2:]:
        copy.wait()


def project_value(noise_level, lookback, latents, level_table, w_query, w_key, w_value, gain_query, gain_key):
    rows, width = latents.shape
    cols = w_query.shape[1]
    half = rows // 2
    main = cols // 256 * 256
    f32, bf16 = jnp.float32, jnp.bfloat16
    operands = (
        noise_level, lookback, latents, level_table, w_query, w_key, w_value, gain_query, gain_key
    )
    operands = [pltpu.with_memory_space_constraint(x, pltpu.HBM) for x in operands]
    return pl.pallas_call(
        value_kernel,
        out_shape=(
            pltpu.VMEM((rows, width), bf16),
            pltpu.VMEM((width, main), bf16),
            pltpu.VMEM((width, 2 * (cols - main)), bf16),
            pltpu.VMEM((cols, rows), bf16),
            pltpu.VMEM((cols + VALUE_PADDING, half), bf16),
            pltpu.VMEM((1, cols), f32),
            pltpu.VMEM((1, cols), f32),
            pltpu.SMEM((3,), jnp.int32),
        ),
        in_specs=[HBM] * 9,
        out_specs=(VMEM,) * 7 + (SMEM,),
        scratch_shapes=[
            pltpu.SMEM((2,), jnp.int32),
            pltpu.SMEM((2,), jnp.int32),
            pltpu.VMEM((rows, width), bf16),
            pltpu.VMEM((width, cols), bf16),
            pltpu.VMEM(level_table.shape, bf16),
            pltpu.VMEM((2, width), f32),
            pltpu.VMEM((2, width), f32),
            pltpu.SemaphoreType.DMA((5,)),
            pltpu.SemaphoreType.DMA((4,)),
            pltpu.SemaphoreType.DMA((5,)),
        ],
        compiler_params=pltpu.CompilerParams(vmem_limit_bytes=22 * MIB),
        cost_estimate=pl.CostEstimate(
            flops=2 * rows * width * cols, bytes_accessed=26_000_000, transcendentals=0
        ),
        name="project_value",
    )(*operands)


def query_key_kernel(shaped, key_weights, mixed_weights, w_query, query, key, sums_out, weights, sem):
    cols = query.shape[1]
    main = key_weights.shape[1]
    rest = cols - main
    fetch = pltpu.make_async_copy(w_query.at[:, pl.ds(rest, main)], weights, sem.at[0])
    fetch.start()

    def dot(w):
        return jnp.dot(shaped[...], w[...], preferred_element_type=jnp.float32)

    key[:, :main] = dot(key_weights)
    middle = dot(mixed_weights)
    key[:, main:] = middle[:, :rest]
    query[:, :rest] = middle[:, rest:]
    fetch.wait()
    query[:, rest:] = dot(weights)
    for at, ref in ((0, key), (4, query)):
        x = ref[...]
        sums_out[at : at + 4, :] = as_rows(jnp.sum(x * x, axis=1, keepdims=True))


def project_query_key(shaped, key_weights, mixed_weights, w_query):
    rows, width = shaped.shape
    cols = w_query.shape[1]
    f32 = jnp.float32
    return pl.pallas_call(
        query_key_kernel,
        out_shape=(
            pltpu.VMEM((rows, cols), f32),
            pltpu.VMEM((rows, cols), f32),
            pltpu.VMEM((8, 128), f32),
        ),
        in_specs=[VMEM] * 3 + [HBM],
        out_specs=(VMEM,) * 3,
        scratch_shapes=[pltpu.VMEM(key_weights.shape, jnp.bfloat16), pltpu.SemaphoreType.DMA((1,))],
        compiler_params=pltpu.CompilerParams(vmem_limit_bytes=16 * MIB),
        cost_estimate=pl.CostEstimate(
            flops=4 * rows * width * cols, bytes_accessed=18_000_000, transcendentals=0
        ),
        name="project_query_key",
    )(shaped, key_weights, mixed_weights, pltpu.with_memory_space_constraint(w_query, pltpu.HBM))


def norm_factor(sums, at, total_cols):
    first, second, third, fourth = (x[at : at + 4, :] for x in sums)
    return as_columns(lax.rsqrt((first + second + (third + fourth)) / total_cols + EPSILON))


def later_kernel(value, out):
    cols, frame = out.shape
    out[...] = value[:cols, frame:]


def later_frame(value, cols):
    return pl.pallas_call(
        later_kernel,
        out_shape=pltpu.VMEM((cols, value.shape[1] // 2), jnp.bfloat16),
        in_specs=[VMEM],
        out_specs=VMEM,
        compiler_params=pltpu.CompilerParams(vmem_limit_bytes=8 * MIB),
        cost_estimate=pl.CostEstimate(flops=1000, bytes_accessed=1000, transcendentals=0),
        name="later_frame",
    )(value)


def key_kernel(total_cols, key, gain, s0, s1, s2, s3, all_out, early, late, passed):
    factor = norm_factor((s0, s1, s2, s3), 0, total_cols)
    half = early.shape[0]
    for c in range(0, key.shape[1], 128):
        normed = (key[:, c : c + 128] * factor * gain[0:1, c : c + 128]).astype(jnp.bfloat16)
        all_out[:, c : c + 128] = normed
        late[:half, c : c + 128] = normed[:half]
        late[half:, c : c + 128] = normed[: 2 * PADDING]
        early[:, c : c + 128] = normed[half:]
        passed[:half, c : c + 128] = normed[half:]
        passed[half:, c : c + 128] = normed[-PADDING:]


def normalise_key(key, gain, sums, total_cols):
    rows, cols = key.shape
    bf16 = jnp.bfloat16
    return pl.pallas_call(
        functools.partial(key_kernel, total_cols),
        out_shape=(
            jax.ShapeDtypeStruct((rows, cols), bf16),
            jax.ShapeDtypeStruct((rows // 2, cols), bf16),
            jax.ShapeDtypeStruct((rows // 2 + 2 * PADDING, cols), bf16),
            jax.ShapeDtypeStruct((rows // 2 + PADDING, cols), bf16),
        ),
        in_specs=[VMEM] * 6,
        out_specs=(VMEM,) * 4,
        compiler_params=pltpu.CompilerParams(vmem_limit_bytes=12 * MIB),
        cost_estimate=pl.CostEstimate(flops=2 * rows * cols, bytes_accessed=100_000, transcendentals=0),
        name="normalise_key",
    )(key, gain, *sums)


def attend_block(first, q, k, vt, acc, peak, mass):
    heads = q.shape[1] // HD
    cols = [slice(h * HD, (h + 1) * HD) for h in range(heads)]
    scores = [
        lax.dot_general(k[:, c], q[:, c], (((1,), (1,)), ((), ())), preferred_element_type=jnp.float32)
        for c in cols
    ]
    tops = [jnp.max(s, axis=0, keepdims=True) for s in scores]
    if not first:
        olds = [peak[h : h + 1, :] for h in range(heads)]
        tops = [jnp.maximum(t, o) for t, o in zip(tops, olds)]
        fades = [jnp.exp2((o - t) * EXP2_SCALE) for t, o in zip(tops, olds)]
    expos = [jnp.exp2((s - t) * EXP2_SCALE) for s, t in zip(scores, tops)]
    for h in range(heads):
        total = jnp.sum(expos[h], axis=0, keepdims=True)
        peak[h : h + 1, :] = tops[h]
        mass[h : h + 1, :] = total if first else mass[h : h + 1, :] * fades[h] + total
    for h, c in enumerate(cols):
        part = jnp.dot(vt[c, :], expos[h].astype(jnp.bfloat16), preferred_element_type=jnp.float32)
        acc[c, :] = part if first else acc[c, :] * fades[h] + part


def local_kernel(
    total_cols, info, query, gain, s0, s1, s2, s3, key, value, query_out, acc, peak, mass,
):
    factor = norm_factor((s0, s1, s2, s3), 4, total_cols)
    for c in range(0, query.shape[1], 128):
        query_out[:, c : c + 128] = (
            query[:, c : c + 128] * factor * gain[0:1, c : c + 128]
        ).astype(jnp.bfloat16)
    frame = query.shape[0] // 2
    at = [pl.ds(0, frame), pl.ds(frame, frame)]
    for f in range(2):
        attend_block(
            True, query_out.at[at[f]], key.at[at[f]], value.at[:, at[f]],
            acc.at[f], peak.at[f], mass.at[f],
        )

    @pl.when(info[1] >= 1)
    def _():
        attend_block(
            False, query_out.at[at[1]], key.at[at[0]], value.at[:, at[0]],
            acc.at[1], peak.at[1], mass.at[1],
        )


def local_attention(info, query, gain, sums, key, value, total_cols):
    rows, cols = query.shape
    f32 = jnp.float32
    return pl.pallas_call(
        functools.partial(local_kernel, total_cols),
        out_shape=(
            pltpu.VMEM((rows, cols), jnp.bfloat16),
            pltpu.VMEM((2, cols, rows // 2), f32),
            pltpu.VMEM((2, 8, rows // 2), f32),
            pltpu.VMEM((2, 8, rows // 2), f32),
        ),
        in_specs=[SMEM] + [VMEM] * 8,
        out_specs=(VMEM,) * 4,
        compiler_params=pltpu.CompilerParams(vmem_limit_bytes=12 * MIB),
        cost_estimate=pl.CostEstimate(flops=3_000_000, bytes_accessed=100_000, transcendentals=0),
        name="local_attention",
    )(info, query, gain, *sums, key, value)


def finish(acc, mass, out):
    for h in range(acc.shape[0] // HD):
        c = slice(h * HD, (h + 1) * HD)
        out[:, c] = jnp.transpose(acc[c, :] / mass[h : h + 1, :]).astype(out.dtype)


def near_kernel(g, info, query, acc_in, peak_in, mass_in, keys, values, acc, peak, mass, *second):
    frame = query.shape[0] // 2
    at = [pl.ds(0, frame), pl.ds(frame, frame)]
    for f in range(2):

        @pl.when(info[f] >= f + 2 - g)
        def _():
            attend_block(
                False, query.at[at[f]], keys.at[at[0]], values.at[:, at[g]],
                acc.at[f], peak.at[f], mass.at[f],
            )

    for out in second:
        finish(acc.at[1], mass.at[1], out)


def near_attention(g, info, query, acc, peak, mass, keys, values):
    rows, cols = query.shape
    f32 = jnp.float32
    second = (pltpu.VMEM((rows // 2, cols), jnp.bfloat16),) if g == 0 else ()
    return pl.pallas_call(
        functools.partial(near_kernel, g),
        out_shape=(
            pltpu.VMEM((2, cols, rows // 2), f32),
            pltpu.VMEM((2, 8, rows // 2), f32),
            pltpu.VMEM((2, 8, rows // 2), f32),
        )
        + second,
        in_specs=[SMEM] + [VMEM] * 6,
        out_specs=(VMEM,) * (3 + len(second)),
        input_output_aliases={2: 0, 3: 1, 4: 2},
        compiler_params=pltpu.CompilerParams(vmem_limit_bytes=12 * MIB),
        cost_estimate=pl.CostEstimate(flops=1_000_000, bytes_accessed=100_000, transcendentals=0),
        name="near_attention",
    )(info, query, acc, peak, mass, keys, values)


def far_kernel(
    info, query, acc_in, peak_in, mass_in, second, far_keys, far_values, relayed_keys, relayed_values,
    out, acc, peak, mass,
):
    frame = query.shape[0] // 2
    at = [pl.ds(0, frame), pl.ds(frame, frame)]
    acc[...] = acc_in[0]
    peak[...] = peak_in[0]
    mass[...] = mass_in[0]
    for core, k, v in (
        (0, far_keys.at[at[0]], far_values),
        (1, relayed_keys, relayed_values),
    ):

        @pl.when(jnp.logical_and(info[2] == core, info[0] >= 3))
        def _():
            attend_block(False, query.at[at[0]], k, v, acc, peak, mass)

    out[at[1], :] = second[...]
    finish(acc, mass, out.at[at[0]])


def far_attention(info, query, acc, peak, mass, second, halo):
    rows, cols = query.shape
    f32 = jnp.float32
    stats = pltpu.VMEM((8, rows // 2), f32)
    return pl.pallas_call(
        far_kernel,
        out_shape=jax.ShapeDtypeStruct((rows, cols), jnp.bfloat16),
        in_specs=[SMEM] + [VMEM] * 9,
        out_specs=VMEM,
        scratch_shapes=[pltpu.VMEM((cols, rows // 2), f32), stats, stats],
        compiler_params=pltpu.CompilerParams(vmem_limit_bytes=12 * MIB),
        cost_estimate=pl.CostEstimate(flops=1_000_000, bytes_accessed=100_000, transcendentals=0),
        name="far_attention",
    )(info, query, acc, peak, mass, second, *halo)


def on_device(
    latents, noise_level, lookback, level_table, w_query, w_key, w_value, gain_query, gain_key
):
    devices = lax.axis_size("queue")
    members = lax.axis_size("tp")
    total_cols = w_query.shape[1] * members
    along = [(i, (i + 1) % devices) for i in range(devices)]
    swap = [(i, i ^ 1) for i in range(devices)]

    def facing(i, t):
        if i in (0, devices - 1):
            return i * members + (t ^ 1)
        return (i + 1 if i % 2 else i - 1) * members + t

    across = [(i * members + t, facing(i, t)) for i in range(devices) for t in range(members)]

    def move(x, pairs):
        return lax.ppermute(x, "queue", pairs)

    def move_across(x):
        return lax.ppermute(x, ("queue", "tp"), across)

    shaped, key_weights, mixed_weights, value, value_early, gain_query, gain_key, info = project_value(
        noise_level, lookback, latents, level_table, w_query, w_key, w_value, gain_query, gain_key
    )
    info = pltpu.with_memory_space_constraint(info, pltpu.SMEM)
    near_value = move(value, along)
    pair_value = move(value_early, swap)
    query, key, sums = project_query_key(shaped, key_weights, mixed_weights, w_query)
    pair_value, sums = lax.optimization_barrier((pair_value, sums))
    sums = [sums] + [
        lax.ppermute(sums, "tp", pairs)
        for pairs in (
            [(0, 1), (1, 0), (2, 3), (3, 2)],
            [(0, 3), (3, 0), (1, 2), (2, 1)],
            [(0, 2), (2, 0), (1, 3), (3, 1)],
        )
    ]
    far_value = move(pair_value, along)
    key_normed, key_early, key_late, key_passed = normalise_key(key, gain_key, sums, total_cols)
    key_normed, near_value = lax.optimization_barrier((key_normed, near_value))
    relayed_value = move(later_frame(near_value, key.shape[1]), swap)
    near_key = move(key_early, along)
    mid_key = move(key_late, along)
    pair_key = move(key_passed, swap)
    far_key = move_across(pair_key)
    key_normed, pair_key = lax.optimization_barrier((key_normed, pair_key))
    query_normed, acc, peak, mass = local_attention(
        info, query, gain_query, sums, key_normed, value, total_cols
    )
    near_key, acc, far_value = lax.optimization_barrier((near_key, acc, far_value))
    relayed_key = move(near_key, swap)
    acc, peak, mass = near_attention(1, info, query_normed, acc, peak, mass, near_key, near_value)
    acc, peak, mass, second = near_attention(
        0, info, query_normed, acc, peak, mass, mid_key, near_value
    )
    return far_attention(
        info, query_normed, acc, peak, mass, second, (far_key, far_value, relayed_key, relayed_value)
    )


def solution(mesh):
    in_specs = (
        P("queue", None),
        P("queue"),
        P("queue"),
        P(),
        P(None, "tp"),
        P(None, "tp"),
        P(None, "tp"),
        P("tp"),
        P("tp"),
    )
    return jax.shard_map(
        on_device, mesh=mesh, in_specs=in_specs, out_specs=P("queue", "tp"), check_vma=False
    )
```

```python
import functools

import jax
import jax.numpy as jnp
from jax import lax
from jax.experimental import pallas as pl
from jax.experimental.pallas import tpu as pltpu
from jax.sharding import PartitionSpec as P

HD = 128
WIN = 4
EPSILON = 1e-06
MIB = 2**20
VALUE_PADDING = 48
PADDING = 8
EXP2_SCALE = HD ** (-0.5) * 1.4426950408889634

HBM = pl.BlockSpec(memory_space=pltpu.HBM)
VMEM = pl.BlockSpec(memory_space=pltpu.VMEM)
SMEM = pl.BlockSpec(memory_space=pltpu.SMEM)


def as_rows(column):
    wide = jnp.broadcast_to(column, (column.shape[0], 128))
    parts = [
        jnp.transpose(wide[i : i + 128])[0:1] for i in range(0, column.shape[0], 128)
    ]
    return jnp.concatenate(parts, 0)


def as_columns(rows):
    parts = [
        jnp.transpose(jnp.broadcast_to(rows[i : i + 1], (128, 128)))
        for i in range(rows.shape[0])
    ]
    return jnp.concatenate(parts, 0)


def value_kernel(
    noise_level, lookback, latents, level_table, w_query, w_key, w_value, gain_query, gain_key,
    shaped, key_weights, mixed_weights, value_both, value_early, gains_query, gains_key, info,
    levels, reaches, lat, weights, table, shift, scale, small_sem, lat_sem, w_sem,
):
    width = latents.shape[1]
    frame = latents.shape[0] // 2
    half = frame // 2
    cols = w_value.shape[1]
    main = key_weights.shape[1]
    rest = cols - main
    small = [
        pltpu.make_async_copy(src, dst, small_sem.at[i])
        for i, (src, dst) in enumerate(
            (
                (noise_level, levels),
                (level_table, table),
                (lookback, reaches),
                (gain_query, gains_query.at[0]),
                (gain_key, gains_key.at[0]),
            )
        )
    ]
    lat_copies = [
        pltpu.make_async_copy(
            latents.at[pl.ds(c * half, half)], lat.at[pl.ds(c * half, half)], lat_sem.at[c]
        )
        for c in range(4)
    ]
    for copy in lat_copies[:1] + small[:2] + lat_copies[1:] + small[2:]:
        copy.start()
    fetches = [
        pltpu.make_async_copy(src, dst, w_sem.at[i])
        for i, (src, dst) in enumerate(
            (
                (w_value.at[:, pl.ds(0, 256)], weights.at[:, pl.ds(0, 256)]),
                (w_value.at[:, pl.ds(256, 384)], weights.at[:, pl.ds(256, 384)]),
                (w_key.at[:, pl.ds(0, main)], key_weights),
                (w_key.at[:, pl.ds(main, rest)], mixed_weights.at[:, pl.ds(0, rest)]),
                (w_query.at[:, pl.ds(0, rest)], mixed_weights.at[:, pl.ds(rest, rest)]),
            )
        )
    ]

    for copy in small[:2]:
        copy.wait()
    pick = lax.broadcasted_iota(jnp.int32, (8, 1), 0)
    wanted = jnp.where(pick == 0, levels[0], levels[1])
    chosen = lax.broadcasted_iota(jnp.int32, (8, table.shape[0]), 1) == wanted
    rows = jnp.dot(
        chosen.astype(jnp.float32).astype(jnp.bfloat16), table[...], preferred_element_type=jnp.float32
    )
    shift[...] = rows[0:2, :width]
    scale[...] = 1.0 + rows[0:2, width:]

    def shape_rows(f, start, count):
        rows = slice(start, start + count)
        x = lat[rows, :].astype(jnp.float32)
        center = jnp.mean(x, axis=1, keepdims=True)
        x = x - center
        spread = jnp.mean(x * x, axis=1, keepdims=True)
        x = x * lax.rsqrt(spread + EPSILON)
        shaped[rows, :] = (x * scale[f : f + 1, :] + shift[f : f + 1, :]).astype(jnp.bfloat16)

    def value_rows(f):
        rows = slice(f * frame, (f + 1) * frame)
        result = jnp.dot(shaped[rows, :], weights[...], preferred_element_type=jnp.float32)
        turned = jnp.transpose(result).astype(jnp.bfloat16)
        value_both[:, rows] = turned
        if f == 1:
            value_early[:cols, :] = turned
            value_early[cols:, :] = turned[:VALUE_PADDING]

    group = 64
    for c in range(2):
        lat_copies[c].wait()
        fetches[c].start()
        for j in range(c * half, (c + 1) * half, group):
            shape_rows(0, j, group)
    for c in range(2, 4):
        lat_copies[c].wait()
        fetches[c].start()
    fetches[4].start()
    fetches[0].wait()
    fetches[1].wait()
    for j in range(frame, 2 * frame, group):
        shape_rows(1, j, group)
    value_rows(0)
    value_rows(1)
    for copy in small[2:]:
        copy.wait()
    info[0] = reaches[0]
    info[1] = reaches[1]
    info[2] = lax.rem(lax.axis_index("queue"), 2)
    for copy in fetches[2:]:
        copy.wait()


def project_value(noise_level, lookback, latents, level_table, w_query, w_key, w_value, gain_query, gain_key):
    rows, width = latents.shape
    cols = w_query.shape[1]
    half = rows // 2
    main = cols // 256 * 256
    f32, bf16 = jnp.float32, jnp.bfloat16
    operands = (
        noise_level, lookback, latents, level_table, w_query, w_key, w_value, gain_query, gain_key
    )
    operands = [pltpu.with_memory_space_constraint(x, pltpu.HBM) for x in operands]
    return pl.pallas_call(
        value_kernel,
        out_shape=(
            pltpu.VMEM((rows, width), bf16),
            pltpu.VMEM((width, main), bf16),
            pltpu.VMEM((width, 2 * (cols - main)), bf16),
            pltpu.VMEM((cols, rows), bf16),
            pltpu.VMEM((cols + VALUE_PADDING, half), bf16),
            pltpu.VMEM((1, cols), f32),
            pltpu.VMEM((1, cols), f32),
            pltpu.SMEM((3,), jnp.int32),
        ),
        in_specs=[HBM] * 9,
        out_specs=(VMEM,) * 7 + (SMEM,),
        scratch_shapes=[
            pltpu.SMEM((2,), jnp.int32),
            pltpu.SMEM((2,), jnp.int32),
            pltpu.VMEM((rows, width), bf16),
            pltpu.VMEM((width, cols), bf16),
            pltpu.VMEM(level_table.shape, bf16),
            pltpu.VMEM((2, width), f32),
            pltpu.VMEM((2, width), f32),
            pltpu.SemaphoreType.DMA((5,)),
            pltpu.SemaphoreType.DMA((4,)),
            pltpu.SemaphoreType.DMA((5,)),
        ],
        compiler_params=pltpu.CompilerParams(vmem_limit_bytes=22 * MIB),
        cost_estimate=pl.CostEstimate(
            flops=2 * rows * width * cols, bytes_accessed=26_000_000, transcendentals=0
        ),
        name="project_value",
    )(*operands)


def query_key_kernel(shaped, key_weights, mixed_weights, w_query, query, key, sums_out, weights, sem):
    cols = query.shape[1]
    main = key_weights.shape[1]
    rest = cols - main
    fetch = pltpu.make_async_copy(w_query.at[:, pl.ds(rest, main)], weights, sem.at[0])
    fetch.start()

    def dot(w):
        return jnp.dot(shaped[...], w[...], preferred_element_type=jnp.float32)

    key[:, :main] = dot(key_weights)
    middle = dot(mixed_weights)
    key[:, main:] = middle[:, :rest]
    query[:, :rest] = middle[:, rest:]
    fetch.wait()
    query[:, rest:] = dot(weights)
    for at, ref in ((0, key), (4, query)):
        x = ref[...]
        sums_out[at : at + 4, :] = as_rows(jnp.sum(x * x, axis=1, keepdims=True))


def project_query_key(shaped, key_weights, mixed_weights, w_query):
    rows, width = shaped.shape
    cols = w_query.shape[1]
    f32 = jnp.float32
    return pl.pallas_call(
        query_key_kernel,
        out_shape=(
            pltpu.VMEM((rows, cols), f32),
            pltpu.VMEM((rows, cols), f32),
            pltpu.VMEM((8, 128), f32),
        ),
        in_specs=[VMEM] * 3 + [HBM],
        out_specs=(VMEM,) * 3,
        scratch_shapes=[pltpu.VMEM(key_weights.shape, jnp.bfloat16), pltpu.SemaphoreType.DMA((1,))],
        compiler_params=pltpu.CompilerParams(vmem_limit_bytes=16 * MIB),
        cost_estimate=pl.CostEstimate(
            flops=4 * rows * width * cols, bytes_accessed=18_000_000, transcendentals=0
        ),
        name="project_query_key",
    )(shaped, key_weights, mixed_weights, pltpu.with_memory_space_constraint(w_query, pltpu.HBM))


def norm_factor(sums, at, total_cols):
    first, second, third, fourth = (x[at : at + 4, :] for x in sums)
    return as_columns(lax.rsqrt((first + second + (third + fourth)) / total_cols + EPSILON))


def later_kernel(value, out):
    cols, frame = out.shape
    out[...] = value[:cols, frame:]


def later_frame(value, cols):
    return pl.pallas_call(
        later_kernel,
        out_shape=pltpu.VMEM((cols, value.shape[1] // 2), jnp.bfloat16),
        in_specs=[VMEM],
        out_specs=VMEM,
        compiler_params=pltpu.CompilerParams(vmem_limit_bytes=8 * MIB),
        cost_estimate=pl.CostEstimate(flops=1000, bytes_accessed=1000, transcendentals=0),
        name="later_frame",
    )(value)


def key_kernel(total_cols, key, gain, s0, s1, s2, s3, all_out, early, late, passed):
    factor = norm_factor((s0, s1, s2, s3), 0, total_cols)
    half = early.shape[0]
    for c in range(0, key.shape[1], 128):
        cut = slice(c, c + 128)
        x = key[:, cut] * factor * gain[0:1, cut]
        all_out[:, cut] = x.astype(jnp.bfloat16)
        early[:, cut] = x[half:].astype(jnp.bfloat16)
        late[:, cut] = jnp.concatenate([x[:half], x[: 2 * PADDING]], 0).astype(jnp.bfloat16)
        passed[:, cut] = jnp.concatenate([x[half:], x[:PADDING]], 0).astype(jnp.bfloat16)


def normalise_key(key, gain, sums, total_cols):
    rows, cols = key.shape
    bf16 = jnp.bfloat16
    return pl.pallas_call(
        functools.partial(key_kernel, total_cols),
        out_shape=(
            jax.ShapeDtypeStruct((rows, cols), bf16),
            jax.ShapeDtypeStruct((rows // 2, cols), bf16),
            jax.ShapeDtypeStruct((rows // 2 + 2 * PADDING, cols), bf16),
            jax.ShapeDtypeStruct((rows // 2 + PADDING, cols), bf16),
        ),
        in_specs=[VMEM] * 6,
        out_specs=(VMEM,) * 4,
        compiler_params=pltpu.CompilerParams(vmem_limit_bytes=12 * MIB),
        cost_estimate=pl.CostEstimate(flops=2 * rows * cols, bytes_accessed=100_000, transcendentals=0),
        name="normalise_key",
    )(key, gain, *sums)


def attend_block(first, q, k, vt, acc, peak, mass):
    heads = q.shape[1] // HD
    cols = [slice(h * HD, (h + 1) * HD) for h in range(heads)]
    scores = [
        lax.dot_general(k[:, c], q[:, c], (((1,), (1,)), ((), ())), preferred_element_type=jnp.float32)
        for c in cols
    ]
    tops = [jnp.max(s, axis=0, keepdims=True) for s in scores]
    if not first:
        olds = [peak[h : h + 1, :] for h in range(heads)]
        tops = [jnp.maximum(t, o) for t, o in zip(tops, olds)]
        fades = [jnp.exp2((o - t) * EXP2_SCALE) for t, o in zip(tops, olds)]
    expos = [jnp.exp2((s - t) * EXP2_SCALE) for s, t in zip(scores, tops)]
    for h in range(heads):
        total = jnp.sum(expos[h], axis=0, keepdims=True)
        peak[h : h + 1, :] = tops[h]
        mass[h : h + 1, :] = total if first else mass[h : h + 1, :] * fades[h] + total
    for h, c in enumerate(cols):
        part = jnp.dot(vt[c, :], expos[h].astype(jnp.bfloat16), preferred_element_type=jnp.float32)
        acc[c, :] = part if first else acc[c, :] * fades[h] + part


def local_kernel(
    total_cols, info, query, gain, s0, s1, s2, s3, key, value, query_out, acc, peak, mass,
):
    factor = norm_factor((s0, s1, s2, s3), 4, total_cols)
    for c in range(0, query.shape[1], 128):
        query_out[:, c : c + 128] = (
            query[:, c : c + 128] * factor * gain[0:1, c : c + 128]
        ).astype(jnp.bfloat16)
    frame = query.shape[0] // 2
    at = [pl.ds(0, frame), pl.ds(frame, frame)]
    for f in range(2):
        attend_block(
            True, query_out.at[at[f]], key.at[at[f]], value.at[:, at[f]],
            acc.at[f], peak.at[f], mass.at[f],
        )

    @pl.when(info[1] >= 1)
    def _():
        attend_block(
            False, query_out.at[at[1]], key.at[at[0]], value.at[:, at[0]],
            acc.at[1], peak.at[1], mass.at[1],
        )


def local_attention(info, query, gain, sums, key, value, total_cols):
    rows, cols = query.shape
    f32 = jnp.float32
    return pl.pallas_call(
        functools.partial(local_kernel, total_cols),
        out_shape=(
            pltpu.VMEM((rows, cols), jnp.bfloat16),
            pltpu.VMEM((2, cols, rows // 2), f32),
            pltpu.VMEM((2, 8, rows // 2), f32),
            pltpu.VMEM((2, 8, rows // 2), f32),
        ),
        in_specs=[SMEM] + [VMEM] * 8,
        out_specs=(VMEM,) * 4,
        compiler_params=pltpu.CompilerParams(vmem_limit_bytes=12 * MIB),
        cost_estimate=pl.CostEstimate(flops=3_000_000, bytes_accessed=100_000, transcendentals=0),
        name="local_attention",
    )(info, query, gain, *sums, key, value)


def finish(acc, mass, out):
    for h in range(acc.shape[0] // HD):
        c = slice(h * HD, (h + 1) * HD)
        out[:, c] = jnp.transpose(acc[c, :] / mass[h : h + 1, :]).astype(out.dtype)


def near_kernel(g, info, query, acc_in, peak_in, mass_in, keys, values, acc, peak, mass, *second):
    frame = query.shape[0] // 2
    at = [pl.ds(0, frame), pl.ds(frame, frame)]
    for f in range(2):

        @pl.when(info[f] >= f + 2 - g)
        def _():
            attend_block(
                False, query.at[at[f]], keys.at[at[0]], values.at[:, at[g]],
                acc.at[f], peak.at[f], mass.at[f],
            )

    for out in second:
        finish(acc.at[1], mass.at[1], out)


def near_attention(g, info, query, acc, peak, mass, keys, values):
    rows, cols = query.shape
    f32 = jnp.float32
    second = (pltpu.VMEM((rows // 2, cols), jnp.bfloat16),) if g == 0 else ()
    return pl.pallas_call(
        functools.partial(near_kernel, g),
        out_shape=(
            pltpu.VMEM((2, cols, rows // 2), f32),
            pltpu.VMEM((2, 8, rows // 2), f32),
            pltpu.VMEM((2, 8, rows // 2), f32),
        )
        + second,
        in_specs=[SMEM] + [VMEM] * 6,
        out_specs=(VMEM,) * (3 + len(second)),
        input_output_aliases={2: 0, 3: 1, 4: 2},
        compiler_params=pltpu.CompilerParams(vmem_limit_bytes=12 * MIB),
        cost_estimate=pl.CostEstimate(flops=1_000_000, bytes_accessed=100_000, transcendentals=0),
        name="near_attention",
    )(info, query, acc, peak, mass, keys, values)


def far_kernel(
    info, query, acc_in, peak_in, mass_in, second, far_keys, far_values, relayed_keys, relayed_values,
    out, acc, peak, mass,
):
    frame = query.shape[0] // 2
    at = [pl.ds(0, frame), pl.ds(frame, frame)]
    acc[...] = acc_in[0]
    peak[...] = peak_in[0]
    mass[...] = mass_in[0]
    for core, k, v in (
        (0, far_keys.at[at[0]], far_values),
        (1, relayed_keys, relayed_values),
    ):

        @pl.when(jnp.logical_and(info[2] == core, info[0] >= 3))
        def _():
            attend_block(False, query.at[at[0]], k, v, acc, peak, mass)

    out[at[1], :] = second[...]
    finish(acc, mass, out.at[at[0]])


def far_attention(info, query, acc, peak, mass, second, halo):
    rows, cols = query.shape
    f32 = jnp.float32
    stats = pltpu.VMEM((8, rows // 2), f32)
    return pl.pallas_call(
        far_kernel,
        out_shape=jax.ShapeDtypeStruct((rows, cols), jnp.bfloat16),
        in_specs=[SMEM] + [VMEM] * 9,
        out_specs=VMEM,
        scratch_shapes=[pltpu.VMEM((cols, rows // 2), f32), stats, stats],
        compiler_params=pltpu.CompilerParams(vmem_limit_bytes=12 * MIB),
        cost_estimate=pl.CostEstimate(flops=1_000_000, bytes_accessed=100_000, transcendentals=0),
        name="far_attention",
    )(info, query, acc, peak, mass, second, *halo)


def on_device(
    latents, noise_level, lookback, level_table, w_query, w_key, w_value, gain_query, gain_key
):
    devices = lax.axis_size("queue")
    members = lax.axis_size("tp")
    total_cols = w_query.shape[1] * members
    along = [(i, (i + 1) % devices) for i in range(devices)]
    swap = [(i, i ^ 1) for i in range(devices)]

    def facing(i, t):
        if i in (0, devices - 1):
            return i * members + (t ^ 1)
        return (i + 1 if i % 2 else i - 1) * members + t

    across = [(i * members + t, facing(i, t)) for i in range(devices) for t in range(members)]

    def move(x, pairs):
        return lax.ppermute(x, "queue", pairs)

    def move_across(x):
        return lax.ppermute(x, ("queue", "tp"), across)

    shaped, key_weights, mixed_weights, value, value_early, gain_query, gain_key, info = project_value(
        noise_level, lookback, latents, level_table, w_query, w_key, w_value, gain_query, gain_key
    )
    info = pltpu.with_memory_space_constraint(info, pltpu.SMEM)
    near_value = move(value, along)
    pair_value = move(value_early, swap)
    query, key, sums = project_query_key(shaped, key_weights, mixed_weights, w_query)
    pair_value, sums = lax.optimization_barrier((pair_value, sums))
    sums = [sums] + [
        lax.ppermute(sums, "tp", pairs)
        for pairs in (
            [(0, 1), (1, 0), (2, 3), (3, 2)],
            [(0, 3), (3, 0), (1, 2), (2, 1)],
            [(0, 2), (2, 0), (1, 3), (3, 1)],
        )
    ]
    far_value = move(pair_value, along)
    key_normed, key_early, key_late, key_passed = normalise_key(key, gain_key, sums, total_cols)
    key_normed, near_value = lax.optimization_barrier((key_normed, near_value))
    relayed_value = move(later_frame(near_value, key.shape[1]), swap)
    near_key = move(key_early, along)
    mid_key = move(key_late, along)
    pair_key = move(key_passed, swap)
    far_key = move_across(pair_key)
    key_normed, pair_key = lax.optimization_barrier((key_normed, pair_key))
    query_normed, acc, peak, mass = local_attention(
        info, query, gain_query, sums, key_normed, value, total_cols
    )
    near_key, acc, far_value = lax.optimization_barrier((near_key, acc, far_value))
    relayed_key = move(near_key, swap)
    acc, peak, mass = near_attention(1, info, query_normed, acc, peak, mass, near_key, near_value)
    acc, peak, mass, second = near_attention(
        0, info, query_normed, acc, peak, mass, mid_key, near_value
    )
    return far_attention(
        info, query_normed, acc, peak, mass, second, (far_key, far_value, relayed_key, relayed_value)
    )


def solution(mesh):
    in_specs = (
        P("queue", None),
        P("queue"),
        P("queue"),
        P(),
        P(None, "tp"),
        P(None, "tp"),
        P(None, "tp"),
        P("tp"),
        P("tp"),
    )
    return jax.shard_map(
        on_device, mesh=mesh, in_specs=in_specs, out_specs=P("queue", "tp"), check_vma=False
    )
```
